256 devices in a mesh: seq: 8 (over x, core), batch: 32 (over z, y).
Axes of the slice: x: 4, y: 4, z: 8, core: 2. Of those that a mesh axis runs over, the one named last changes fastest.
Arguments:
- patches: bfloat16 [32, 2560, 1280], P('batch', 'seq'), may hold values from -30 to 30
- window_ids: int32 [32, 640], P('batch', 'seq'), may hold values from 0 to 79, never falling along the last dimension, each value on 1 to 16 neighbouring positions
- norm_gain: float32 [1280], replicated, may hold values from 0.1 to 1.9
- w_qkv: bfloat16 [3, 1280, 1280], P(None, None, 'seq'), may hold values from -2 to 2
- b_qkv: float32 [3, 1280], replicated, may hold values from -3 to 3
- w_proj: bfloat16 [1280, 1280], P('seq'), may hold values from -0.15625 to 0.15625
- b_proj: float32 [1280], replicated, may hold values from -3 to 3
- merge_gain: float32 [1280], replicated, may hold values from 0.1 to 1.9
- token_lists: int32 [20480], replicated, may hold values from 0 to 20479, as said below
- req_owner: int32 [128], replicated, may hold values from 0 to 31, as said below
- req_counts: int32 [128], replicated, may hold values from 1 to 319, as said below
Outputs:
- cache: bfloat16 [32, 1276, 5120], P('batch', None, 'seq')
The draws below stay inside these ranges and needn't reach their ends.
Inputs may be any that keep to these rules, and one draw needn't show every extreme that they name: `token_lists`: a permutation of the merged tokens; the merged tokens of one group that fall in one owner's requests number at most 40. `req_owner`: each owner holds exactly 4 requests. `req_counts`: they sum to 20480.
All inputs are finite; a program needn't handle non-finite values.
Results may differ from the reference program's by a relative error of at most 0.005.
Values may be sent and summed in bfloat16 or wider, within the bound.
A program may use at most 128 MiB of HBM per device.

```python
import math
import jax
import jax.numpy as jnp
import numpy as np
from jax import lax

W = 1280
HEADS = 16
WIN = 64
REQS = 4
HD = 80
MW = 5120
HALO = 63
SEQLEN = 2560
GROUP = 640
TOKENS = 20480
WINDOWS = 80
REQUESTS = 128
MEANREQ = 160
MOST = 319
CAP = 1276
N_BATCH = 32


def layout(key):
    subkeys = jax.random.split(key, 6)
    half_count = REQUESTS // 2
    canonical = jnp.arange(REQUESTS, dtype=jnp.int32)
    canon_owner = canonical // REQS
    busiest = jax.random.randint(subkeys[1], (), 0, N_BATCH)
    firsts = jax.random.randint(subkeys[0], (half_count,), 1, 2 * MEANREQ)
    firsts = jnp.where(canon_owner[:half_count] == busiest, 2 * MEANREQ - 1, jnp.where(canon_owner[half_count:] == busiest, 1, firsts))
    sizes = jnp.concatenate([firsts, 2 * MEANREQ - firsts]).astype(jnp.int32)
    request_perm = jax.random.permutation(subkeys[2], REQUESTS).astype(jnp.int32)
    owner_perm = jax.random.permutation(subkeys[3], N_BATCH).astype(jnp.int32)
    counts = jnp.zeros((REQUESTS,), jnp.int32).at[request_perm].set(sizes)
    owner_of_id = jnp.zeros((REQUESTS,), jnp.int32).at[request_perm].set(canon_owner)
    owners = owner_perm[owner_of_id]
    ends = jnp.cumsum(counts).astype(jnp.int32)
    starts = ends - counts
    slots = jnp.arange(TOKENS, dtype=jnp.int32)
    inside = (slots[:, None] >= starts[None, :]) & (slots[:, None] < ends[None, :])
    ids_list = jnp.arange(REQUESTS, dtype=jnp.int32)
    request_of = jnp.sum(jnp.where(inside, ids_list[None, :], 0), axis=1)
    within = slots - jnp.sum(jnp.where(inside, starts[None, :], 0), axis=1)
    earlier = (owner_of_id[:, None] == owner_of_id[None, :]) & (ids_list[None, :] < ids_list[:, None])
    request_offset = jnp.sum(jnp.where(earlier, counts[None, :], 0), axis=1)
    loads = jnp.zeros((N_BATCH,), jnp.int32).at[canon_owner].add(sizes)
    owner_start = jnp.cumsum(loads).astype(jnp.int32) - loads
    sequence_index = owner_start[owner_of_id[request_of]] + request_offset[request_of] + within
    group_perm = jax.random.permutation(subkeys[4], N_BATCH).astype(jnp.int32)
    groups = group_perm[sequence_index % N_BATCH]
    positions = sequence_index // N_BATCH
    local_perm = jax.vmap(lambda sub: jax.random.permutation(sub, GROUP))(jax.random.split(subkeys[5], N_BATCH)).astype(jnp.int32)
    token_ids = groups * GROUP + local_perm[groups, positions]
    return (token_ids.astype(jnp.int32), owners.astype(jnp.int32), counts.astype(jnp.int32))


def draw_token_lists(key, part):
    token_ids, owners, counts = layout(key)
    return token_ids


def draw_req_owner(key, part):
    token_ids, owners, counts = layout(key)
    return owners


def draw_req_counts(key, part):
    token_ids, owners, counts = layout(key)
    return counts


def draw_patches(key, part):
    key = jax.random.fold_in(key, 11)
    subkeys = jax.random.split(key, 4)
    full_shape = (N_BATCH, SEQLEN, W)
    values = jax.random.normal(subkeys[0], full_shape, jnp.float32)
    row_scale = jnp.exp(jax.random.uniform(subkeys[2], (N_BATCH, SEQLEN, 1), jnp.float32, jnp.log(0.3), jnp.log(3.0)))
    column_scale = jnp.exp(jax.random.uniform(subkeys[3], (W,), jnp.float32, jnp.log(0.3), jnp.log(3.0)))
    return jnp.clip(values * row_scale * column_scale, -30.0, 30.0).astype(jnp.bfloat16)


def draw_w_qkv(key, part):
    key = jax.random.fold_in(key, 12)
    subkeys = jax.random.split(key, 1)
    spread = W ** (-0.5)
    stacked = spread * jax.random.normal(subkeys[0], (3, W, W), jnp.float32)
    return jnp.clip(stacked, -2.0, 2.0).astype(jnp.bfloat16)


def shard_levels(stream_key, dims, pieces, smallest, largest):
    def one(axis_at, shards_of):
        heights = jax.random.uniform(jax.random.fold_in(jax.random.fold_in(stream_key, 6), axis_at), (shards_of,), jnp.float32, smallest / len(pieces), largest / len(pieces))
        return jnp.repeat(jnp.exp(heights), dims[axis_at] // shards_of).reshape((-1,) + (1,) * (len(dims) - axis_at - 1))

    loudness = one(*pieces[0])
    for cut in pieces[1:]:
        loudness = loudness * one(*cut)
    return loudness


def profile(number_of, total, bound, skew):
    portions = [(1 << 20) // math.isqrt(rank ** skew) + 1 for rank in range(2, number_of + 1)]
    spare, holding = total - bound - (number_of - 1), [1] * (number_of - 1)
    while spare > 0:
        movable = [i for i in range(number_of - 1) if holding[i] < bound]
        whole, remaining = sum([portions[i] for i in movable]), spare
        for i in movable:
            more = min(bound - holding[i], max(1, remaining * portions[i] // whole), spare)
            holding[i] = holding[i] + more
            spare = spare - more
    return np.array([bound] + holding)


def ragged(own_key, number_of, total, limit, slope):
    if number_of == 2:
        one = jax.random.randint(own_key, (), max(1, total - limit), min(limit, total - 1) + 1)
        return jnp.stack([one, total - one])
    lengths = jnp.asarray(profile(number_of, total, limit, slope), jnp.int32)
    pairs = (number_of - 1) // 2
    donor, taker = lengths[1:1 + 2 * pairs:2], lengths[2:2 + 2 * pairs:2]
    room = jnp.minimum(donor - 1, limit - taker)
    passed = jax.random.randint(jax.random.fold_in(own_key, 1), (pairs,), 0, 1 << 20) % (room + 1)
    lengths = lengths.at[1:1 + 2 * pairs:2].set(donor - passed).at[2:2 + 2 * pairs:2].set(taker + passed)
    return lengths[jax.random.permutation(jax.random.fold_in(own_key, 2), number_of)]


def normal_values(key, shape, width, bound, cuts=(), kind=jnp.bfloat16):
    result = width * jax.random.normal(key, shape, jnp.float32)
    if cuts:
        result = result * shard_levels(key, shape, cuts, -0.22, 0.18)
    return jnp.clip(result, -bound, bound).astype(kind)


def setup_inputs(seed: int = 0) -> dict:
    arg_keys = jax.random.split(jax.random.key(seed), 12)
    patches = draw_patches(jax.random.fold_in(arg_keys[11], 71), 0)
    window_ids = jax.vmap(lambda own: jnp.searchsorted(jnp.cumsum(ragged(own, WINDOWS, GROUP, WIN // 4, 2)), jnp.arange(GROUP), side="right"))(jax.random.split(arg_keys[1], N_BATCH)).reshape((N_BATCH, GROUP)).astype(jnp.int32)
    norm_gain = jnp.clip(1.0 + 0.18 * jax.random.normal(arg_keys[2], (W,), jnp.float32), 0.1, 1.9)
    w_qkv = draw_w_qkv(jax.random.fold_in(arg_keys[11], 71), 0)
    b_qkv = normal_values(arg_keys[4], (3, W), 0.5, 3.0, (), jnp.float32)
    w_proj = normal_values(arg_keys[5], (W, W), W ** -0.5, 0.15625, ((0, 8),))
    b_proj = normal_values(arg_keys[6], (W,), 0.5, 3.0, (), jnp.float32)
    merge_gain = jnp.clip(1.0 + 0.18 * jax.random.normal(arg_keys[7], (W,), jnp.float32), 0.1, 1.9)
    token_lists = draw_token_lists(jax.random.fold_in(arg_keys[11], 71), 0)
    req_owner = draw_req_owner(jax.random.fold_in(arg_keys[11], 71), 0)
    req_counts = draw_req_counts(jax.random.fold_in(arg_keys[11], 71), 0)
    return dict(patches=patches, window_ids=window_ids, norm_gain=norm_gain, w_qkv=w_qkv, b_qkv=b_qkv, w_proj=w_proj, b_proj=b_proj, merge_gain=merge_gain, token_lists=token_lists, req_owner=req_owner, req_counts=req_counts)


def rms_scaled(values, gain):
    return values * lax.rsqrt(lax.optimization_barrier(jnp.mean(values * values, axis=-1, keepdims=True)) + 1e-06) * gain

def band_attend(queries, keys_band, values_band, query_ids, key_ids, margin):
    row_count = queries.shape[0]
    block_rows = min(512, row_count)
    block_count = row_count // block_rows
    band_width = block_rows + 2 * margin
    scaling = 1.0 / math.sqrt(queries.shape[2])

    def one_block(block_index):
        starting = (block_index * block_rows).astype(jnp.int32)
        query_block = lax.dynamic_slice_in_dim(queries, starting, block_rows, 0).astype(jnp.float32)
        key_block = lax.dynamic_slice_in_dim(keys_band, starting, band_width, 0).astype(jnp.float32)
        value_block = lax.dynamic_slice_in_dim(values_band, starting, band_width, 0).astype(jnp.float32)
        own_ids = lax.dynamic_slice_in_dim(query_ids, starting, block_rows, 0)
        other_ids = lax.dynamic_slice_in_dim(key_ids, starting, band_width, 0)
        matches = own_ids[:, None] == other_ids[None, :]
        scores = jnp.einsum('qhd,khd->hqk', query_block, key_block) * scaling
        scores = jnp.where(matches[None], scores, -1e+30)
        maxima = lax.optimization_barrier(jnp.max(scores, axis=2, keepdims=True))
        exponent = jnp.exp(scores - maxima)
        weights = (exponent / lax.optimization_barrier(jnp.sum(exponent, axis=2, keepdims=True))).astype(jnp.bfloat16)
        mixed = jnp.einsum('hqk,khd->qhd', weights.astype(jnp.float32), value_block)
        return mixed.astype(jnp.bfloat16)
    attended = lax.map(one_block, jnp.arange(block_count, dtype=jnp.int32))
    return attended.reshape(row_count, -1)

def reference(patches, window_ids, norm_gain, w_qkv, b_qkv, w_proj, b_proj, merge_gain, token_lists, req_owner, req_counts):

    def encode(group_args):
        group_rows, unit_ids = group_args
        group_ids = jnp.repeat(unit_ids, 4)
        rows_float = group_rows.astype(jnp.float32)
        normalized = rms_scaled(rows_float, norm_gain).astype(jnp.bfloat16)
        projected = [(jnp.dot(normalized, w_qkv[which], preferred_element_type=jnp.float32) + b_qkv[which]).astype(jnp.bfloat16) for which in range(3)]
        widths = ((HALO, HALO), (0, 0), (0, 0))
        queries = projected[0].reshape(SEQLEN, HEADS, HD)
        keys_band = jnp.pad(projected[1].reshape(SEQLEN, HEADS, HD), widths)
        values_band = jnp.pad(projected[2].reshape(SEQLEN, HEADS, HD), widths)
        padded_ids = jnp.pad(group_ids, (HALO, HALO), constant_values=-1)
        attended = band_attend(queries, keys_band, values_band, group_ids, padded_ids, HALO)
        resid = rows_float + jnp.dot(attended, w_proj, preferred_element_type=jnp.float32) + b_proj
        normed = rms_scaled(resid, merge_gain)
        return normed.reshape(GROUP, MW).astype(jnp.bfloat16)
    merged = lax.map(encode, (patches, window_ids)).reshape(TOKENS, MW)
    ends = jnp.cumsum(req_counts).astype(jnp.int32)
    starts = (ends - req_counts).astype(jnp.int32)
    slots = jnp.arange(TOKENS, dtype=jnp.int32)
    request_of = jnp.searchsorted(ends, slots, side='right').astype(jnp.int32)
    requests = jnp.arange(REQUESTS, dtype=jnp.int32)
    same_owner = req_owner[None, :] == req_owner[:, None]
    ranks = lax.optimization_barrier(jnp.sum(same_owner & (requests[None, :] < requests[:, None]), axis=1)).astype(jnp.int32)
    target = req_owner[request_of] * CAP + ranks[request_of] * MOST + slots - starts[request_of]
    cache = jnp.zeros((N_BATCH * CAP, MW), jnp.bfloat16).at[target.astype(jnp.int32)].set(merged[token_lists])
    return cache.reshape(N_BATCH, CAP, MW)
```

```python
import math

import jax
import jax.numpy as jnp
from jax import lax
from jax.experimental import pallas as pl
from jax.experimental.pallas import tpu as pltpu
from jax.sharding import PartitionSpec as P

HEADS = 16
REQS = 4
HALO = 63
SLOTS = 40
GROUP = 640
TOKENS = 20480
MOST = 319
CAP = 1276
ROWS = 1280
PER = 8


def rms_scaled(values, gain):
    return values * lax.rsqrt(jnp.mean(values * values, axis=-1, keepdims=True) + 1e-06) * gain


def band_attend(queries, keys_band, values_band, query_ids, key_ids, margin):
    row_count = queries.shape[0]
    block_rows = min(512, row_count)
    block_count = row_count // block_rows
    band_width = block_rows + 2 * margin
    scaling = 1.0 / math.sqrt(queries.shape[2])

    def one_block(block_index):
        starting = block_index * block_rows
        query_block = lax.dynamic_slice_in_dim(queries, starting, block_rows, 0)
        key_block = lax.dynamic_slice_in_dim(keys_band, starting, band_width, 0)
        value_block = lax.dynamic_slice_in_dim(values_band, starting, band_width, 0)
        own_ids = lax.dynamic_slice_in_dim(query_ids, starting, block_rows, 0)
        other_ids = lax.dynamic_slice_in_dim(key_ids, starting, band_width, 0)
        matches = own_ids[:, None] == other_ids[None, :]
        scores = (
            jnp.einsum("qhd,khd->hqk", query_block, key_block, preferred_element_type=jnp.float32)
            * scaling
        )
        scores = jnp.where(matches[None], scores, -1e30)
        maxima = jnp.max(scores, axis=2, keepdims=True)
        exponent = jnp.exp(scores - maxima)
        weights = (exponent / jnp.sum(exponent, axis=2, keepdims=True)).astype(jnp.bfloat16)
        mixed = jnp.einsum("hqk,khd->qhd", weights, value_block, preferred_element_type=jnp.float32)
        return mixed.astype(jnp.bfloat16)

    attended = lax.map(one_block, jnp.arange(block_count, dtype=jnp.int32))
    return attended.reshape(row_count, -1)


def attend_sequence(qkv_rows, head_count, padded_ids, query_ids):
    row_count = qkv_rows.shape[0]
    head_size = qkv_rows.shape[2] // head_count
    widths = ((HALO, HALO), (0, 0), (0, 0))
    queries = qkv_rows[:, 0].reshape(row_count, head_count, head_size)
    keys_band = jnp.pad(qkv_rows[:, 1].reshape(row_count, head_count, head_size), widths)
    values_band = jnp.pad(qkv_rows[:, 2].reshape(row_count, head_count, head_size), widths)
    return band_attend(queries, keys_band, values_band, query_ids, padded_ids, HALO)


def routing_tables(token_lists, req_owner, req_counts, group, owner):
    ends = jnp.cumsum(req_counts)
    starts = ends - req_counts
    slots = jnp.arange(TOKENS, dtype=jnp.int32)
    inside = (slots[:, None] >= starts[None, :]) & (slots[:, None] < ends[None, :])
    slot_owner = jnp.sum(jnp.where(inside, req_owner[None, :], 0), axis=1)
    local = jnp.arange(GROUP, dtype=jnp.int32)
    owner_of = jnp.sum(
        jnp.where(token_lists[:, None] == group * GROUP + local[None, :], slot_owner[:, None], 0), axis=0
    )
    before = (owner_of[:, None] == owner_of[None, :]) & (local[:, None] < local[None, :])
    send_slot = owner_of * SLOTS + jnp.sum(before, axis=0, dtype=jnp.int32)
    requests = jnp.arange(req_owner.shape[0], dtype=jnp.int32)
    own = req_owner == owner
    own_rank = jnp.sum(own[:, None] & (requests[:, None] < requests[None, :]), axis=0)
    padded = jnp.concatenate([token_lists, jnp.zeros((MOST + 1,), jnp.int32)])
    held = []
    for rank in range(REQS):
        chosen = own & (own_rank == rank)
        start = jnp.sum(jnp.where(chosen, starts, 0))
        count = jnp.sum(jnp.where(chosen, req_counts, 0))
        listed = lax.dynamic_slice(padded, (start,), (MOST,))
        held.append(jnp.where(jnp.arange(MOST) < count, listed, -1))
    held.append(jnp.full((ROWS - CAP,), -1, jnp.int32))
    tokens = jnp.concatenate(held)
    first = (tokens // GROUP) * GROUP
    earlier = (tokens[:, None] < tokens[None, :]) & (tokens[:, None] >= first[None, :])
    taken = jnp.sum(earlier, axis=0, dtype=jnp.int32)
    source = jnp.where(tokens >= 0, (tokens // GROUP) * SLOTS + taken, -1)
    return send_slot[None, :], source[:, None]


def route_kernel(slot_ref, source_ref, merged_ref, cache_ref, packed, landed, total, send_sem, land_sem):
    n_batch = lax.axis_size("batch")
    me = lax.axis_index("batch")
    barrier = pltpu.get_barrier_semaphore()

    @pl.loop(1, n_batch)
    def _(step):
        pl.semaphore_signal(barrier, inc=1, device_id={"batch": lax.rem(me + step, n_batch)})

    pl.semaphore_wait(barrier, n_batch - 1)

    def copy(step):
        return pltpu.make_async_remote_copy(
            src_ref=packed.at[step],
            dst_ref=landed.at[step],
            send_sem=send_sem.at[step],
            recv_sem=land_sem.at[step],
            device_id={"batch": lax.rem(me + step, n_batch)},
        )

    @pl.loop(0, n_batch // PER)
    def _(part):
        for inner in range(PER):
            step = part * PER + inner
            owner = lax.rem(me + step, n_batch)
            wanted = lax.broadcasted_iota(jnp.int32, (SLOTS, GROUP), 0) + owner * SLOTS
            picks = jnp.where(slot_ref[...] == wanted, 1.0, 0.0).astype(jnp.bfloat16)
            rows = jnp.dot(picks, merged_ref[...], preferred_element_type=jnp.float32)
            packed[step] = rows.astype(jnp.bfloat16)
        for inner in range(PER):
            step = part * PER + inner

            @pl.when(step > 0)
            def _():
                copy(step).start()

    landed[0] = packed[0]

    for part in range(n_batch // PER):
        marks = []
        blocks = []
        for inner in range(PER):
            step = part * PER + inner
            if step > 0:
                copy(step).wait_recv()
            blocks.append(landed[step])
            group = lax.rem(me - step + n_batch, n_batch)
            marks.append(lax.broadcasted_iota(jnp.int32, (1, SLOTS), 1) + group * SLOTS)
        marks = jnp.concatenate(marks, axis=1)
        blocks = jnp.concatenate(blocks, axis=0)

        @pl.loop(0, ROWS // 256)
        def _(tile):
            rows = pl.ds(pl.multiple_of(tile * 256, 256), 256)
            picks = jnp.where(source_ref[rows, :] == marks, 1.0, 0.0).astype(jnp.bfloat16)
            placed = jnp.dot(picks, blocks, preferred_element_type=jnp.float32)
            if part == 0:
                total[rows, :] = placed
            else:
                total[rows, :] += placed

    cache_ref[...] = total[:CAP, :].astype(jnp.bfloat16)

    @pl.loop(1, n_batch)
    def _(step):
        copy(step).wait_send()


def route(send_slot, source, merged):
    n_batch = lax.axis_size("batch")
    features = merged.shape[1]
    vmem = pl.BlockSpec(memory_space=pltpu.VMEM)
    return pl.pallas_call(
        route_kernel,
        out_shape=jax.ShapeDtypeStruct((CAP, features), jnp.bfloat16),
        in_specs=[vmem] * 3,
        out_specs=vmem,
        scratch_shapes=[
            pltpu.VMEM((n_batch, SLOTS, features), jnp.bfloat16),
            pltpu.VMEM((n_batch, SLOTS, features), jnp.bfloat16),
            pltpu.VMEM((ROWS, features), jnp.float32),
            pltpu.SemaphoreType.DMA((n_batch,)),
            pltpu.SemaphoreType.DMA((n_batch,)),
        ],
        compiler_params=pltpu.CompilerParams(
            collective_id=0, has_side_effects=True, vmem_limit_bytes=40 * 1024 * 1024
        ),
    )(send_slot, source, merged)


def shards(
    patches,
    window_ids,
    norm_gain,
    w_qkv,
    b_qkv,
    w_proj,
    b_proj,
    merge_gain,
    token_lists,
    req_owner,
    req_counts,
):
    seq_count = lax.axis_size("seq")
    batch_place = lax.axis_index("batch")
    patch_rows = patches[0]
    rows_here = patch_rows.shape[0]
    width = patch_rows.shape[1]
    rows_float = patch_rows.astype(jnp.float32)
    normalized = rms_scaled(rows_float, norm_gain).astype(jnp.bfloat16)
    unit_ids = lax.all_gather(window_ids, "seq", axis=1, tiled=True)[0]
    group_ids = jnp.repeat(unit_ids, 4)
    padded_ids = jnp.pad(group_ids, (HALO, HALO), constant_values=-1)
    product = jnp.einsum(
        "rw,iwc->ric",
        normalized,
        lax.all_gather(w_qkv, "seq", axis=2, tiled=True),
        preferred_element_type=jnp.float32,
    )
    qkv_own = (product + b_qkv[None]).astype(jnp.bfloat16)
    qkv_group = lax.all_to_all(qkv_own, "seq", split_axis=2, concat_axis=0, tiled=True)
    attended_local = attend_sequence(qkv_group, HEADS // seq_count, padded_ids, group_ids)
    attended_own = lax.all_to_all(attended_local, "seq", split_axis=0, concat_axis=1, tiled=True)
    projected = jnp.dot(
        attended_own,
        lax.all_gather(w_proj, "seq", axis=0, tiled=True),
        preferred_element_type=jnp.float32,
    )
    resid = rows_float + projected + b_proj
    normed = rms_scaled(resid, merge_gain)
    merged = normed.reshape(rows_here // 4, 4 * width).astype(jnp.bfloat16)
    grouped = lax.all_to_all(merged, "seq", split_axis=1, concat_axis=0, tiled=True)
    send_slot, source = routing_tables(token_lists, req_owner, req_counts, batch_place, batch_place)
    return route(send_slot, source, grouped)[None]


def solution(mesh):
    return jax.shard_map(
        shards,
        mesh=mesh,
        in_specs=(
            P("batch", "seq", None),
            P("batch", "seq"),
            P(),
            P(None, None, "seq"),
            P(),
            P("seq", None),
            P(),
            P(),
            P(),
            P(),
            P(),
        ),
        out_specs=P("batch", None, "seq"),
        check_vma=False,
    )
```

```python
import math

import jax
import jax.numpy as jnp
from jax import lax
from jax.experimental import pallas as pl
from jax.experimental.pallas import tpu as pltpu
from jax.sharding import PartitionSpec as P

REQS = 4
WIDTH = 1280
TALL = 2688
SCALE = math.log2(math.e) / math.sqrt(80)
SLOTS = 40
GROUP = 640
TOKENS = 20480
MOST = 319
CAP = 1276
ROWS = 1280
PER = 8


def dot(left, right, dims=((1,), (0,))):
    return lax.dot_general(left, right, (dims, ((), ())), preferred_element_type=jnp.float32)


def iota(shape, axis):
    return lax.broadcasted_iota(jnp.int32, shape, axis)


def onehot(condition):
    return jnp.where(condition, 1.0, 0.0).astype(jnp.bfloat16)


def encode_kernel(
    patch_ref, ids_ref, gain_ref, w_ref, b_ref, wproj_ref, bproj_ref, merge_ref, merged_ref,
    raw, xn, wt, bias, q, kv, perm, id_send, id_land, id_row, id_col, attn, pieces, mixed, wp, resid,
    sums_out, sums_in, x_send, x_land, d_send, d_land, i_send, i_land, ws_sem, wx_sem, wy_sem,
    a_send, a_land, f_send, f_land, s_sem,
):
    place = lax.axis_index("seq")
    batch = lax.axis_index("batch")
    x, core = place // 2, place % 2
    row_y = batch % 4
    column = batch - row_y
    sibling = place + 1 - 2 * core
    right = lax.rem(x + 1, 4) * 2 + core
    left = lax.rem(x + 3, 4) * 2 + core
    barrier = pltpu.get_barrier_semaphore()

    for step in range(1, 8):
        pl.semaphore_signal(barrier, inc=1, device_id={"seq": lax.rem(place + step, 8)})
    for step in range(1, 4):
        pl.semaphore_signal(barrier, inc=1, device_id={"batch": column + lax.rem(row_y + step, 4)})
    pl.semaphore_wait(barrier, 10)

    def rows_of(chip, half=None):
        start = lax.rem(chip, 4) * 640 + core * 320
        if half is None:
            return pl.ds(pl.multiple_of(start, 32), 320)
        return pl.ds(pl.multiple_of(start + half * 160, 32), 160)

    def remote(src, dst, send, land, **device):
        return pltpu.make_async_remote_copy(
            src_ref=src, dst_ref=dst, send_sem=send, recv_sem=land, device_id=device
        )

    def ring(which):
        half = (0, 1, 1, 0, 0, 1)[which]
        target = (right, left, right, left, right, left)[which]
        if which < 4:
            src = patch_ref.at[pl.ds(half * 160, 160), :]
            dst = raw.at[rows_of(x, half), :]
        else:
            rows = rows_of(x + 3 if which == 4 else x + 1, half)
            src, dst = raw.at[rows, :], raw.at[rows, :]
        return remote(src, dst, x_send.at[which], x_land.at[which], seq=target)

    def share(which):
        if which == 6:
            return remote(patch_ref, raw.at[rows_of(x), :], d_send.at[6], d_land.at[6], seq=sibling)
        chip = x + (3, 1, 3, 1, 2, 2)[which]
        rows = rows_of(chip, (0, 1, 1, 0, 0, 1)[which])
        return remote(raw.at[rows, :], raw.at[rows, :], d_send.at[which], d_land.at[which], seq=sibling)

    def id_copy(step):
        return remote(
            id_send, id_land.at[place], i_send.at[step], i_land.at[step], seq=lax.rem(place + step, 8)
        )

    own_wrows = pl.ds(pl.multiple_of(place * 160, 32), 160)

    def wp_swap():
        columns = pl.ds(pl.multiple_of((1 - core) * 640, 128), 640)
        return remote(wproj_ref.at[:, columns], wp.at[own_wrows, :], ws_sem.at[0], ws_sem.at[1], seq=sibling)

    def wp_part(chip):
        return pl.ds(pl.multiple_of(lax.rem(chip, 4) * 320 + row_y * 80, 16), 80)

    def wp_x(dx):
        rows = wp_part(x)
        target = lax.rem(x + dx, 4) * 2 + core
        return remote(wp.at[rows, :], wp.at[rows, :], wx_sem.at[0, dx - 1], wx_sem.at[1, dx - 1], seq=target)

    def wp_y(dx, dy):
        rows = wp_part(x + 4 - dx)
        index = (dx - 1) * 3 + dy - 1
        return remote(
            wp.at[rows, :], wp.at[rows, :], wy_sem.at[0, index], wy_sem.at[1, index],
            batch=column + lax.rem(row_y + dy, 4),
        )

    id_send[...] = jnp.zeros_like(id_send)
    id_send[0:1, 0:80] = ids_ref[...]
    share(6).start()
    ring(0).start()
    ring(1).start()
    for step in range(1, 8):
        id_copy(step).start()
    wp_swap().start()
    ring(2).start()
    ring(3).start()

    wp[own_wrows, :] = wproj_ref[:, pl.ds(pl.multiple_of(core * 640, 128), 640)]
    raw[rows_of(x), :] = patch_ref[...]
    id_land[place] = id_send[...]
    xn[0:64, :] = jnp.zeros((64, WIDTH), jnp.bfloat16)
    xn[TALL - 64 : TALL, :] = jnp.zeros((64, WIDTH), jnp.bfloat16)
    identity = onehot(iota((160, 160), 0) == iota((160, 160), 1))
    for which in range(3):
        rows = pl.ds(which * 160, 160)
        wt[rows, :] = dot(identity, w_ref[which], ((1,), (1,))).astype(jnp.bfloat16)
        lanes = iota((160, WIDTH), 1) == iota((160, WIDTH), 0) + place * 160
        picked = jnp.sum(jnp.where(lanes, b_ref[which : which + 1, :], 0.0), axis=1, keepdims=True)
        bias[rows, :] = jnp.broadcast_to(picked, (160, 128))
    inner = iota((512, 512), 1)
    perm[...] = onehot(iota((512, 512), 0) == (inner & 127) * 4 + (inner >> 7))

    def project(first, count, xrow, columns, out, out_row, wide):
        del wide
        product = dot(wt[first : first + count, :], xn[xrow, :], ((1,), (1,)))
        product = product + bias[first : first + count, 0:1]
        out[out_row : out_row + count, columns] = product.astype(jnp.bfloat16)

    def attend(block):
        own = pl.ds(pl.multiple_of(block * 128, 128), 128)
        band = pl.ds(pl.multiple_of(block * 128, 128), 256)
        matches = id_col[band, :] == id_row[0:1, own]
        for head in range(2):
            feats = pl.ds(head * 80, 80)
            scores = dot(kv[feats, band], q[feats, own], ((0,), (0,)))
            scores = jnp.where(matches, scores, -1e30)
            peak = jnp.max(scores, axis=0, keepdims=True)
            weights = jnp.exp2((scores - peak) * SCALE)
            total = jnp.sum(weights, axis=0, keepdims=True)
            out = dot(kv[pl.ds(160 + head * 80, 80), band], weights.astype(jnp.bfloat16))
            attn[feats, own] = (out * (1.0 / total)).astype(jnp.bfloat16)

    def take_chip(chip):
        chip = lax.rem(chip, 4)
        base = chip * 640

        @pl.loop(0, 10)
        def _(tile):
            start = pl.multiple_of(base + tile * 64, 64)
            rows = raw[pl.ds(start, 64), :].astype(jnp.float32)
            level = lax.rsqrt(jnp.mean(rows * rows, axis=1, keepdims=True) + 1e-06)
            xn[pl.ds(pl.multiple_of(start + 64, 64), 64), :] = (rows * level * gain_ref[...]).astype(jnp.bfloat16)

        project(
            0, 160, pl.ds(pl.multiple_of(base + 64, 64), 640), pl.ds(pl.multiple_of(base, 128), 640), q, 0, 640
        )
        wide = pl.ds(pl.multiple_of(base + 128, 128), 512)
        project(160, 320, wide, wide, kv, 0, 512)

        units = jnp.concatenate([id_land[chip * 2, 0:1, :], id_land[chip * 2 + 1, 0:1, :]], axis=1)
        units = units.astype(jnp.float32).astype(jnp.bfloat16)
        spread = iota((640, 256), 0)
        spread = onehot(jnp.where(spread < 320, spread >> 2, ((spread - 320) >> 2) + 128) == iota((640, 256), 1))
        id_row[:, pl.ds(pl.multiple_of(base, 128), 640)] = dot(
            jnp.broadcast_to(units, (8, 256)), spread, ((1,), (1,))
        )
        id_col[pl.ds(pl.multiple_of(base + 64, 64), 640), :] = dot(
            spread, jnp.broadcast_to(units, (128, 256)), ((1,), (1,))
        )

        @pl.loop(1, 4)
        def _(tile):
            attend(chip * 5 + tile)

    id_col[0:64, :] = jnp.full((64, 128), -1.0, jnp.float32)
    id_col[TALL - 64 : TALL, :] = jnp.full((64, 128), -1.0, jnp.float32)
    for step in range(1, 8):
        id_copy(step).wait_recv()
    share(6).wait_recv()
    wp_swap().wait_recv()
    for dx in range(1, 4):
        wp_x(dx).start()
    take_chip(x)
    for which in (0, 1):
        ring(which).wait_recv()
        ring(which + 4).start()
        share(which).start()
    for dx in range(1, 4):
        wp_x(dx).wait_recv()
        for dy in range(1, 4):
            wp_y(dx, dy).start()
    for which in (2, 3):
        ring(which).wait_recv()
        share(which).start()
    share(0).wait_recv()
    share(2).wait_recv()
    take_chip(x + 3)
    share(1).wait_recv()
    share(3).wait_recv()
    take_chip(x + 1)
    for which in (4, 5):
        ring(which).wait_recv()
        share(which).start()
    for which in (4, 5):
        share(which).wait_recv()
    take_chip(x + 2)

    @pl.loop(0, 5)
    def _(edge):
        columns = pl.ds(pl.multiple_of(edge * 640, 128), 128)
        project(160, 320, columns, columns, kv, 0, 128)

    @pl.loop(0, 4)
    def _(chip):
        attend(chip * 5)
        attend(chip * 5 + 4)

    def chunk_of(part):
        return pl.ds(pl.multiple_of(part * 128, 128), 128)

    def feats_of(chip, at):
        return pl.ds(pl.multiple_of(lax.rem(chip, 4) * 320 + at * 160, 32), 160)

    def a_copy(dx, part):
        chip = lax.rem(x + dx, 4)
        return remote(
            pieces.at[chip, :, chunk_of(part)],
            mixed.at[feats_of(x, core), chunk_of(part)],
            a_send.at[dx - 1, part],
            a_land.at[dx - 1, part],
            seq=chip * 2 + core,
        )

    def a_share(dx, part):
        block = mixed.at[feats_of(x + 4 - dx, core), chunk_of(part)]
        return remote(block, block, f_send.at[dx, part], f_land.at[dx, part], seq=sibling)

    @pl.loop(0, 5)
    def _(part):
        chunk = attn[:, pl.ds(pl.multiple_of(part * 512, 128), 512)]
        sorted_rows = dot(chunk, perm[...]).astype(jnp.bfloat16)
        for k in range(4):
            pieces[k, :, chunk_of(part)] = sorted_rows[:, k * 128 : k * 128 + 128]
        for dx in (2, 1, 3):
            a_copy(dx, part).start()
        mixed[feats_of(x, core), chunk_of(part)] = pieces[x, :, chunk_of(part)]
        a_share(0, part).start()

    half = pl.ds(pl.multiple_of(core * 640, 128), 640)
    pick = onehot(iota((128, 512), 1) == iota((128, 512), 0) * 4 + x)

    @pl.loop(0, 5)
    def _(part):
        rows = raw[pl.ds(pl.multiple_of(part * 512, 128), 512), half]
        resid[chunk_of(part), :] = dot(pick, rows) + bproj_ref[:, half]

    for dx in range(1, 4):
        for dy in range(1, 4):
            wp_y(dx, dy).wait_recv()

    def s_copy(part):
        return remote(
            sums_out.at[chunk_of(part), :], sums_in.at[chunk_of(part), :], s_sem.at[0, part], s_sem.at[1, part],
            seq=sibling,
        )

    @pl.loop(0, 5)
    def _(part):
        for dx in (1, 3, 2):
            a_copy(dx, part).wait_recv()
            a_share(dx, part).start()
        for dx in (0, 1, 3, 2):
            a_share(dx, part).wait_recv()
        rows = resid[chunk_of(part), :] + dot(mixed[:, chunk_of(part)], wp[...], ((0,), (0,)))
        resid[chunk_of(part), :] = rows
        total = jnp.sum(rows * rows, axis=1, keepdims=True)
        sums_out[chunk_of(part), :] = jnp.broadcast_to(total, (128, 128))
        s_copy(part).start()

    @pl.loop(0, 5)
    def _(part):
        s_copy(part).wait_recv()
        total = sums_out[chunk_of(part), 0:1] + sums_in[chunk_of(part), 0:1]
        level = lax.rsqrt(total * (1.0 / WIDTH) + 1e-06)
        merged_ref[chunk_of(part), :] = (resid[chunk_of(part), :] * level * merge_ref[:, half]).astype(jnp.bfloat16)

    for which in range(6):
        ring(which).wait_send()
    for which in range(7):
        share(which).wait_send()
    for step in range(1, 8):
        id_copy(step).wait_send()
    wp_swap().wait_send()
    for dx in range(1, 4):
        wp_x(dx).wait_send()
        for dy in range(1, 4):
            wp_y(dx, dy).wait_send()

    @pl.loop(0, 5)
    def _(part):
        for dx in range(1, 4):
            a_copy(dx, part).wait_send()
        for dx in range(4):
            a_share(dx, part).wait_send()
        s_copy(part).wait_send()


def encode(patches, ids, norm_gain, w_qkv, b_qkv, w_proj, b_proj, merge_gain):
    vmem = pl.BlockSpec(memory_space=pltpu.VMEM)
    dma = pltpu.SemaphoreType.DMA
    bf16, f32 = jnp.bfloat16, jnp.float32
    return pl.pallas_call(
        encode_kernel,
        out_shape=jax.ShapeDtypeStruct((GROUP, GROUP), bf16),
        in_specs=[vmem] * 8,
        out_specs=vmem,
        scratch_shapes=[
            pltpu.VMEM((2560, WIDTH), bf16),
            pltpu.VMEM((TALL, WIDTH), bf16),
            pltpu.VMEM((480, WIDTH), bf16),
            pltpu.VMEM((480, 128), f32),
            pltpu.VMEM((160, 2560), bf16),
            pltpu.VMEM((320, TALL), bf16),
            pltpu.VMEM((512, 512), bf16),
            pltpu.VMEM((8, 128), jnp.int32),
            pltpu.VMEM((8, 8, 128), jnp.int32),
            pltpu.VMEM((8, 2560), f32),
            pltpu.VMEM((TALL, 128), f32),
            pltpu.VMEM((160, 2560), bf16),
            pltpu.VMEM((4, 160, GROUP), bf16),
            pltpu.VMEM((WIDTH, GROUP), bf16),
            pltpu.VMEM((WIDTH, GROUP), bf16),
            pltpu.VMEM((GROUP, GROUP), f32),
            pltpu.VMEM((GROUP, 128), f32),
            pltpu.VMEM((GROUP, 128), f32),
            dma((6,)), dma((6,)), dma((7,)), dma((7,)), dma((8,)), dma((8,)),
            dma((2,)), dma((2, 3)), dma((2, 9)),
            dma((3, 5)), dma((3, 5)), dma((4, 5)), dma((4, 5)), dma((2, 5)),
        ],
        compiler_params=pltpu.CompilerParams(
            collective_id=1, has_side_effects=True, vmem_limit_bytes=56 * 1024 * 1024
        ),
    )(patches, ids, norm_gain, w_qkv, b_qkv, w_proj, b_proj, merge_gain)


def routing_tables(token_lists, req_owner, req_counts, group, owner):
    ends = jnp.cumsum(req_counts)
    starts = ends - req_counts
    slots = jnp.arange(TOKENS, dtype=jnp.int32)
    inside = (slots[:, None] >= starts[None, :]) & (slots[:, None] < ends[None, :])
    slot_owner = jnp.sum(jnp.where(inside, req_owner[None, :], 0), axis=1)
    local = jnp.arange(GROUP, dtype=jnp.int32)
    owner_of = jnp.sum(
        jnp.where(token_lists[:, None] == group * GROUP + local[None, :], slot_owner[:, None], 0), axis=0
    )
    before = (owner_of[:, None] == owner_of[None, :]) & (local[:, None] < local[None, :])
    send_slot = owner_of * SLOTS + jnp.sum(before, axis=0, dtype=jnp.int32)
    requests = jnp.arange(req_owner.shape[0], dtype=jnp.int32)
    own = req_owner == owner
    own_rank = jnp.sum(own[:, None] & (requests[:, None] < requests[None, :]), axis=0)
    padded = jnp.concatenate([token_lists, jnp.zeros((MOST + 1,), jnp.int32)])
    held = []
    for rank in range(REQS):
        chosen = own & (own_rank == rank)
        start = jnp.sum(jnp.where(chosen, starts, 0))
        count = jnp.sum(jnp.where(chosen, req_counts, 0))
        listed = lax.dynamic_slice(padded, (start,), (MOST,))
        held.append(jnp.where(jnp.arange(MOST) < count, listed, -1))
    held.append(jnp.full((ROWS - CAP,), -1, jnp.int32))
    tokens = jnp.concatenate(held)
    first = (tokens // GROUP) * GROUP
    earlier = (tokens[:, None] < tokens[None, :]) & (tokens[:, None] >= first[None, :])
    taken = jnp.sum(earlier, axis=0, dtype=jnp.int32)
    source = jnp.where(tokens >= 0, (tokens // GROUP) * SLOTS + taken, -1)
    return send_slot[None, :], source[:, None]


def route_kernel(slot_ref, source_ref, merged_ref, cache_ref, packed, landed, total, send_sem, land_sem):
    n_batch = lax.axis_size("batch")
    me = lax.axis_index("batch")
    barrier = pltpu.get_barrier_semaphore()

    @pl.loop(1, n_batch)
    def _(step):
        pl.semaphore_signal(barrier, inc=1, device_id={"batch": lax.rem(me + step, n_batch)})

    pl.semaphore_wait(barrier, n_batch - 1)

    def copy(step):
        return pltpu.make_async_remote_copy(
            src_ref=packed.at[step],
            dst_ref=landed.at[step],
            send_sem=send_sem.at[step],
            recv_sem=land_sem.at[step],
            device_id={"batch": lax.rem(me + step, n_batch)},
        )

    @pl.loop(0, n_batch // PER)
    def _(part):
        for inner in range(PER):
            step = part * PER + inner
            owner = lax.rem(me + step, n_batch)
            wanted = lax.broadcasted_iota(jnp.int32, (SLOTS, GROUP), 0) + owner * SLOTS
            picks = jnp.where(slot_ref[...] == wanted, 1.0, 0.0).astype(jnp.bfloat16)
            rows = jnp.dot(picks, merged_ref[...], preferred_element_type=jnp.float32)
            packed[step] = rows.astype(jnp.bfloat16)
        for inner in range(PER):
            step = part * PER + inner

            @pl.when(step > 0)
            def _():
                copy(step).start()

    landed[0] = packed[0]

    for part in range(n_batch // PER):
        marks = []
        blocks = []
        for inner in range(PER):
            step = part * PER + inner
            if step > 0:
                copy(step).wait_recv()
            blocks.append(landed[step])
            group = lax.rem(me - step + n_batch, n_batch)
            marks.append(lax.broadcasted_iota(jnp.int32, (1, SLOTS), 1) + group * SLOTS)
        marks = jnp.concatenate(marks, axis=1)
        blocks = jnp.concatenate(blocks, axis=0)

        @pl.loop(0, ROWS // 256)
        def _(tile):
            rows = pl.ds(pl.multiple_of(tile * 256, 256), 256)
            picks = jnp.where(source_ref[rows, :] == marks, 1.0, 0.0).astype(jnp.bfloat16)
            placed = jnp.dot(picks, blocks, preferred_element_type=jnp.float32)
            if part == 0:
                total[rows, :] = placed
            else:
                total[rows, :] += placed

    cache_ref[...] = total[:CAP, :].astype(jnp.bfloat16)

    @pl.loop(1, n_batch)
    def _(step):
        copy(step).wait_send()


def route(send_slot, source, merged):
    n_batch = lax.axis_size("batch")
    features = merged.shape[1]
    vmem = pl.BlockSpec(memory_space=pltpu.VMEM)
    return pl.pallas_call(
        route_kernel,
        out_shape=jax.ShapeDtypeStruct((CAP, features), jnp.bfloat16),
        in_specs=[vmem] * 3,
        out_specs=vmem,
        scratch_shapes=[
            pltpu.VMEM((n_batch, SLOTS, features), jnp.bfloat16),
            pltpu.VMEM((n_batch, SLOTS, features), jnp.bfloat16),
            pltpu.VMEM((ROWS, features), jnp.float32),
            pltpu.SemaphoreType.DMA((n_batch,)),
            pltpu.SemaphoreType.DMA((n_batch,)),
        ],
        compiler_params=pltpu.CompilerParams(
            collective_id=0, has_side_effects=True, vmem_limit_bytes=40 * 1024 * 1024
        ),
    )(send_slot, source, merged)


def shards(
    patches, window_ids, norm_gain, w_qkv, b_qkv, w_proj, b_proj, merge_gain, token_lists, req_owner, req_counts
):
    batch_place = lax.axis_index("batch")
    merged = encode(
        patches[0], window_ids, norm_gain[None], w_qkv, b_qkv, w_proj, b_proj[None], merge_gain[None]
    )
    send_slot, source = routing_tables(token_lists, req_owner, req_counts, batch_place, batch_place)
    return route(send_slot, source, merged)[None]


def solution(mesh):
    return jax.shard_map(
        shards,
        mesh=mesh,
        in_specs=(
            P("batch", "seq", None),
            P("batch", "seq"),
            P(),
            P(None, None, "seq"),
            P(),
            P("seq", None),
            P(),
            P(),
            P(),
            P(),
            P(),
        ),
        out_specs=P("batch", None, "seq"),
        check_vma=False,
    )
```

```python
import math

import jax
import jax.numpy as jnp
from jax import lax
from jax.experimental import pallas as pl
from jax.experimental.pallas import tpu as pltpu
from jax.sharding import PartitionSpec as P

REQS = 4
WIDTH = 1280
TALL = 2688
SCALE = math.log2(math.e) / math.sqrt(80)
SLOTS = 40
GROUP = 640
MOST = 319
CAP = 1276
ROWS = 1280
PER = 8


def dot(left, right, dims=((1,), (0,))):
    return lax.dot_general(left, right, (dims, ((), ())), preferred_element_type=jnp.float32)


def iota(shape, axis):
    return lax.broadcasted_iota(jnp.int32, shape, axis)


def onehot(condition):
    return jnp.where(condition, 1.0, 0.0).astype(jnp.bfloat16)


def lanes_of(ref, first, count):
    return jnp.concatenate([ref[pl.ds(first + at, 1), :] for at in range(count)], axis=1)


def tables(tok_ref, owner_ref, count_ref, batch, steps, jumps, owners, dests, slot, source):
    f32 = jnp.float32
    me = batch.astype(f32)
    counts = count_ref[...].astype(f32)
    owner = owner_ref[...].astype(f32)

    def flip(row):
        return jnp.transpose(jnp.broadcast_to(row, (128, 128)))

    lower = iota((128, 128), 0) < iota((128, 128), 1)
    owner_down = flip(owner)
    starts = jnp.sum(jnp.where(lower, flip(counts), 0.0), axis=0, keepdims=True)
    ranks = jnp.sum(jnp.where(lower & (owner_down == owner), 1.0, 0.0), axis=0, keepdims=True)
    steps[...] = flip(starts)
    previous = jnp.where(iota((128, 128), 0) == 0, 0.0, pltpu.roll(owner_down, 1, 0))
    jumps[...] = owner_down - previous
    places = (iota((160, 128), 0) * 128 + iota((160, 128), 1)).astype(f32)

    def jump(request, held):
        return held + jnp.where(places >= steps[pl.ds(request, 1), :], jumps[pl.ds(request, 1), :], 0.0)

    owners[...] = lax.fori_loop(0, 128, jump, jnp.zeros((160, 128), f32), unroll=4)
    dest = jnp.zeros((160, 128), f32)
    for rank in range(REQS):
        chosen = (owner == me) & (ranks == rank)
        start = jnp.sum(jnp.where(chosen, starts, 0.0), axis=1, keepdims=True)
        count = jnp.sum(jnp.where(chosen, counts, 0.0), axis=1, keepdims=True)
        within = (places >= start) & (places < start + count)
        dest = dest + jnp.where(within, places - start + (MOST * rank + 1), 0.0)
    dests[...] = dest.astype(jnp.int32) - 1

    def gather(part, sums):
        rows = pl.ds(pl.multiple_of(part * 8, 8), 8)
        token = tok_ref[rows, :]
        local = token - batch * GROUP
        dest = dests[rows, :]
        owner = owners[rows, :] + 1.0
        high = (token >> 7).astype(f32) + 1.0
        low = (token & 127).astype(f32)
        down, short = iota((128, 128), 0), iota((16, 128), 0)
        group_left, group_right, own_left, own_right = [], [], [], []
        for at in range(8):
            row = slice(at, at + 1)
            group_left.append(onehot(down == (local[row] & 127)))
            group_right.append(jnp.where(short == (local[row] >> 7), owner[row], 0.0).astype(jnp.bfloat16))
            own_left.append(onehot(down == (dest[row] & 127)))
            mine = short == (dest[row] >> 7)
            own_right.append(
                jnp.concatenate([jnp.where(mine, high[row], 0.0), jnp.where(mine, low[row], 0.0)], axis=0).astype(
                    jnp.bfloat16
                )
            )
        first = dot(jnp.concatenate(group_left, axis=1), jnp.concatenate(group_right, axis=1), ((1,), (1,)))
        second = dot(jnp.concatenate(own_left, axis=1), jnp.concatenate(own_right, axis=1), ((1,), (1,)))
        return sums[0] + first, sums[1] + second

    owner_cols, token_cols = lax.fori_loop(
        0, 20, gather, (jnp.zeros((128, 16), f32), jnp.zeros((128, 32), f32))
    )
    unit = onehot(iota((128, 128), 0) == iota((128, 128), 1))
    owner_rows = dot(owner_cols.astype(jnp.bfloat16), unit, ((0,), (0,)))
    token_rows = dot(token_cols.astype(jnp.bfloat16), unit, ((0,), (0,)))

    owner_row = jnp.concatenate([owner_rows[at : at + 1] for at in range(5)], axis=1)
    before = jnp.zeros((1, GROUP), f32)
    for at in range(5):
        same = (owner_cols[:, at : at + 1] == owner_row) & (
            iota((128, GROUP), 0) + at * 128 < iota((128, GROUP), 1)
        )
        before = before + jnp.sum(jnp.where(same, 1.0, 0.0), axis=0, keepdims=True)
    slot[...] = jnp.broadcast_to((owner_row - 1.0) * SLOTS + before, (8, GROUP))

    token_row = jnp.concatenate(
        [(token_rows[at : at + 1] - 1.0) * 128 + token_rows[at + 16 : at + 17] for at in range(10)], axis=1
    )
    for at in range(10):
        high = token_cols[:, at : at + 1] - 1.0
        token = high * 128 + token_cols[:, at + 16 : at + 17]
        group = jnp.floor((high + 0.5) * 0.2)
        earlier = jnp.where((token_row < token) & (token_row >= group * GROUP), 1.0, 0.0)
        taken = jnp.sum(earlier, axis=1, keepdims=True)
        found = jnp.where(high >= 0.0, group * SLOTS + taken, -1.0)
        source[at * 128 : at * 128 + 128, :] = jnp.broadcast_to(found, (128, 128))


def encode_kernel(
    patch_ref, ids_ref, gain_ref, wt, b_ref, wproj_ref, bproj_ref, merge_ref, tok_ref, owner_ref, count_ref,
    cache_ref, merged_ref, steps, jumps, owners, dests, slot, source, packed, landed, total_ref, send_sem, land_sem,
    raw, xn, bias, q, kv, perm, id_send, id_land, id_row, id_col, attn, pieces, mixed, wp, resid,
    sums_out, sums_in, x_send, x_land, d_send, d_land, i_send, i_land, ws_sem, wx_sem, wy_sem,
    a_send, a_land, f_send, f_land, s_sem,
):
    place = lax.axis_index("seq")
    batch = lax.axis_index("batch")
    n_batch = lax.axis_size("batch")
    x, core = place // 2, place % 2
    row_y = batch % 4
    column = batch - row_y
    sibling = place + 1 - 2 * core
    right = lax.rem(x + 1, 4) * 2 + core
    left = lax.rem(x + 3, 4) * 2 + core
    barrier = pltpu.get_barrier_semaphore()

    for step in range(1, 8):
        pl.semaphore_signal(barrier, inc=1, device_id={"seq": lax.rem(place + step, 8)})

    @pl.loop(1, n_batch)
    def _(step):
        pl.semaphore_signal(barrier, inc=1, device_id={"batch": lax.rem(batch + step, n_batch)})

    pl.semaphore_wait(barrier, 7 + n_batch - 1)

    def rows_of(chip, half=None):
        start = lax.rem(chip, 4) * 640 + core * 320
        if half is None:
            return pl.ds(pl.multiple_of(start, 32), 320)
        return pl.ds(pl.multiple_of(start + half * 160, 32), 160)

    def remote(src, dst, send, land, **device):
        return pltpu.make_async_remote_copy(
            src_ref=src, dst_ref=dst, send_sem=send, recv_sem=land, device_id=device
        )

    def ring(which):
        half = (0, 1, 1, 0, 0, 1)[which]
        target = (right, left, right, left, right, left)[which]
        if which < 4:
            src = patch_ref.at[pl.ds(half * 160, 160), :]
            dst = raw.at[rows_of(x, half), :]
        else:
            rows = rows_of(x + 3 if which == 4 else x + 1, half)
            src, dst = raw.at[rows, :], raw.at[rows, :]
        return remote(src, dst, x_send.at[which], x_land.at[which], seq=target)

    def share(which):
        if which == 6:
            return remote(patch_ref, raw.at[rows_of(x), :], d_send.at[6], d_land.at[6], seq=sibling)
        chip = x + (3, 1, 3, 1, 2, 2)[which]
        rows = rows_of(chip, (0, 1, 1, 0, 0, 1)[which])
        return remote(raw.at[rows, :], raw.at[rows, :], d_send.at[which], d_land.at[which], seq=sibling)

    def id_copy(step):
        return remote(
            id_send, id_land.at[place], i_send.at[step], i_land.at[step], seq=lax.rem(place + step, 8)
        )

    own_wrows = pl.ds(pl.multiple_of(place * 160, 32), 160)

    def wp_swap():
        columns = pl.ds(pl.multiple_of((1 - core) * 640, 128), 640)
        return remote(wproj_ref.at[:, columns], wp.at[own_wrows, :], ws_sem.at[0], ws_sem.at[1], seq=sibling)

    def wp_part(chip):
        return pl.ds(pl.multiple_of(lax.rem(chip, 4) * 320 + row_y * 80, 16), 80)

    def wp_x(dx):
        rows = wp_part(x)
        target = lax.rem(x + dx, 4) * 2 + core
        return remote(wp.at[rows, :], wp.at[rows, :], wx_sem.at[0, dx - 1], wx_sem.at[1, dx - 1], seq=target)

    def wp_y(dx, dy):
        rows = wp_part(x + 4 - dx)
        index = (dx - 1) * 3 + dy - 1
        return remote(
            wp.at[rows, :], wp.at[rows, :], wy_sem.at[0, index], wy_sem.at[1, index],
            batch=column + lax.rem(row_y + dy, 4),
        )

    id_send[...] = jnp.zeros_like(id_send)
    id_send[0:1, 0:80] = ids_ref[...]
    share(6).start()
    ring(0).start()
    ring(1).start()
    for step in range(1, 8):
        id_copy(step).start()
    wp_swap().start()
    ring(2).start()
    ring(3).start()

    wp[own_wrows, :] = wproj_ref[:, pl.ds(pl.multiple_of(core * 640, 128), 640)]
    raw[rows_of(x), :] = patch_ref[...]
    id_land[place] = id_send[...]
    xn[0:64, :] = jnp.zeros((64, WIDTH), jnp.bfloat16)
    xn[TALL - 64 : TALL, :] = jnp.zeros((64, WIDTH), jnp.bfloat16)
    for which in range(3):
        rows = pl.ds(which * 160, 160)
        lanes = iota((160, WIDTH), 1) == iota((160, WIDTH), 0) + place * 160
        picked = jnp.sum(jnp.where(lanes, b_ref[which : which + 1, :], 0.0), axis=1, keepdims=True)
        bias[rows, :] = jnp.broadcast_to(picked, (160, 128))
    inner = iota((512, 512), 1)
    perm[...] = onehot(iota((512, 512), 0) == (inner & 127) * 4 + (inner >> 7))

    def project(first, count, xrow, columns, out, out_row, wide):
        del wide
        product = dot(wt[first : first + count, :], xn[xrow, :], ((1,), (1,)))
        product = product + bias[first : first + count, 0:1]
        out[out_row : out_row + count, columns] = product.astype(jnp.bfloat16)

    def attend(block):
        own = pl.ds(pl.multiple_of(block * 128, 128), 128)
        band = pl.ds(pl.multiple_of(block * 128, 128), 256)
        matches = id_col[band, :] == id_row[0:1, own]
        for head in range(2):
            feats = pl.ds(head * 80, 80)
            scores = dot(kv[feats, band], q[feats, own], ((0,), (0,)))
            scores = jnp.where(matches, scores, -1e30)
            peak = jnp.max(scores, axis=0, keepdims=True)
            weights = jnp.exp2((scores - peak) * SCALE)
            total = jnp.sum(weights, axis=0, keepdims=True)
            out = dot(kv[pl.ds(160 + head * 80, 80), band], weights.astype(jnp.bfloat16))
            attn[feats, own] = (out * (1.0 / total)).astype(jnp.bfloat16)

    def take_chip(chip):
        chip = lax.rem(chip, 4)
        base = chip * 640
        gain = lanes_of(gain_ref, 0, 10)

        @pl.loop(0, 10)
        def _(tile):
            start = pl.multiple_of(base + tile * 64, 64)
            rows = raw[pl.ds(start, 64), :].astype(jnp.float32)
            level = lax.rsqrt(jnp.mean(rows * rows, axis=1, keepdims=True) + 1e-06)
            xn[pl.ds(pl.multiple_of(start + 64, 64), 64), :] = (rows * level * gain).astype(jnp.bfloat16)

        project(
            0, 160, pl.ds(pl.multiple_of(base + 64, 64), 640), pl.ds(pl.multiple_of(base, 128), 640), q, 0, 640
        )
        wide = pl.ds(pl.multiple_of(base + 128, 128), 512)
        project(160, 320, wide, wide, kv, 0, 512)

        units = jnp.concatenate([id_land[chip * 2, 0:1, :], id_land[chip * 2 + 1, 0:1, :]], axis=1)
        units = units.astype(jnp.float32).astype(jnp.bfloat16)
        spread = iota((640, 256), 0)
        spread = onehot(jnp.where(spread < 320, spread >> 2, ((spread - 320) >> 2) + 128) == iota((640, 256), 1))
        id_row[:, pl.ds(pl.multiple_of(base, 128), 640)] = dot(
            jnp.broadcast_to(units, (8, 256)), spread, ((1,), (1,))
        )
        id_col[pl.ds(pl.multiple_of(base + 64, 64), 640), :] = dot(
            spread, jnp.broadcast_to(units, (128, 256)), ((1,), (1,))
        )

        @pl.loop(1, 4)
        def _(tile):
            attend(chip * 5 + tile)

    tables(tok_ref, owner_ref, count_ref, batch, steps, jumps, owners, dests, slot, source)
    id_col[0:64, :] = jnp.full((64, 128), -1.0, jnp.float32)
    id_col[TALL - 64 : TALL, :] = jnp.full((64, 128), -1.0, jnp.float32)
    for step in range(1, 8):
        id_copy(step).wait_recv()
    share(6).wait_recv()
    wp_swap().wait_recv()
    for dx in range(1, 4):
        wp_x(dx).start()
    take_chip(x)
    for which in (0, 1):
        ring(which).wait_recv()
        ring(which + 4).start()
        share(which).start()
    for dx in range(1, 4):
        wp_x(dx).wait_recv()
        for dy in range(1, 4):
            wp_y(dx, dy).start()
    for which in (2, 3):
        ring(which).wait_recv()
        share(which).start()
    share(0).wait_recv()
    share(2).wait_recv()
    take_chip(x + 3)
    share(1).wait_recv()
    share(3).wait_recv()
    take_chip(x + 1)
    for which in (4, 5):
        ring(which).wait_recv()
        share(which).start()
    for which in (4, 5):
        share(which).wait_recv()
    take_chip(x + 2)

    @pl.loop(0, 5)
    def _(edge):
        columns = pl.ds(pl.multiple_of(edge * 640, 128), 128)
        project(160, 320, columns, columns, kv, 0, 128)

    @pl.loop(0, 4)
    def _(chip):
        attend(chip * 5)
        attend(chip * 5 + 4)

    def chunk_of(part):
        return pl.ds(pl.multiple_of(part * 128, 128), 128)

    def feats_of(chip, at):
        return pl.ds(pl.multiple_of(lax.rem(chip, 4) * 320 + at * 160, 32), 160)

    def a_copy(dx, part):
        chip = lax.rem(x + dx, 4)
        return remote(
            pieces.at[chip, :, chunk_of(part)],
            mixed.at[feats_of(x, core), chunk_of(part)],
            a_send.at[dx - 1, part],
            a_land.at[dx - 1, part],
            seq=chip * 2 + core,
        )

    def a_share(dx, part):
        block = mixed.at[feats_of(x + 4 - dx, core), chunk_of(part)]
        return remote(block, block, f_send.at[dx, part], f_land.at[dx, part], seq=sibling)

    @pl.loop(0, 5)
    def _(part):
        chunk = attn[:, pl.ds(pl.multiple_of(part * 512, 128), 512)]
        sorted_rows = dot(chunk, perm[...]).astype(jnp.bfloat16)
        for k in range(4):
            pieces[k, :, chunk_of(part)] = sorted_rows[:, k * 128 : k * 128 + 128]
        for dx in (2, 1, 3):
            a_copy(dx, part).start()
        mixed[feats_of(x, core), chunk_of(part)] = pieces[x, :, chunk_of(part)]
        a_share(0, part).start()

    half = pl.ds(pl.multiple_of(core * 640, 128), 640)
    pick = onehot(iota((128, 512), 1) == iota((128, 512), 0) * 4 + x)

    @pl.loop(0, 5)
    def _(part):
        rows = raw[pl.ds(pl.multiple_of(part * 512, 128), 512), half]
        resid[chunk_of(part), :] = dot(pick, rows) + lanes_of(bproj_ref, core * 5, 5)

    for dx in range(1, 4):
        for dy in range(1, 4):
            wp_y(dx, dy).wait_recv()

    def s_copy(part):
        return remote(
            sums_out.at[chunk_of(part), :], sums_in.at[chunk_of(part), :], s_sem.at[0, part], s_sem.at[1, part],
            seq=sibling,
        )

    @pl.loop(0, 5)
    def _(part):
        for dx in (1, 3, 2):
            a_copy(dx, part).wait_recv()
            a_share(dx, part).start()
        for dx in (0, 1, 3, 2):
            a_share(dx, part).wait_recv()
        rows = resid[chunk_of(part), :] + dot(mixed[:, chunk_of(part)], wp[...], ((0,), (0,)))
        resid[chunk_of(part), :] = rows
        total = jnp.sum(rows * rows, axis=1, keepdims=True)
        sums_out[chunk_of(part), :] = jnp.broadcast_to(total, (128, 128))
        s_copy(part).start()

    @pl.loop(0, 5)
    def _(part):
        s_copy(part).wait_recv()
        total = sums_out[chunk_of(part), 0:1] + sums_in[chunk_of(part), 0:1]
        level = lax.rsqrt(total * (1.0 / WIDTH) + 1e-06)
        merged_ref[chunk_of(part), :] = (resid[chunk_of(part), :] * level * lanes_of(merge_ref, core * 5, 5)).astype(jnp.bfloat16)

    def copy(step):
        return pltpu.make_async_remote_copy(
            src_ref=packed.at[step],
            dst_ref=landed.at[step],
            send_sem=send_sem.at[step],
            recv_sem=land_sem.at[step],
            device_id={"batch": lax.rem(batch + step, n_batch)},
        )

    @pl.loop(0, n_batch // PER)
    def _(part):
        for inner in range(PER):
            step = part * PER + inner
            owner = lax.rem(batch + step, n_batch)
            wanted = (iota((SLOTS, GROUP), 0) + owner * SLOTS).astype(jnp.float32)
            picks = onehot(slot[0:1, :] == wanted)
            rows = dot(picks, merged_ref[...])
            packed[step] = rows.astype(jnp.bfloat16)
        for inner in range(PER):
            step = part * PER + inner

            @pl.when(step > 0)
            def _():
                copy(step).start()

    landed[0] = packed[0]

    for part in range(n_batch // PER):
        marks = []
        blocks = []
        for inner in range(PER):
            step = part * PER + inner
            if step > 0:
                copy(step).wait_recv()
            blocks.append(landed[step])
            group = lax.rem(batch - step + n_batch, n_batch)
            marks.append((iota((1, SLOTS), 1) + group * SLOTS).astype(jnp.float32))
        marks = jnp.concatenate(marks, axis=1)
        blocks = jnp.concatenate(blocks, axis=0)

        @pl.loop(0, ROWS // 256)
        def _(tile):
            rows = pl.ds(pl.multiple_of(tile * 256, 256), 256)
            picks = onehot(source[rows, 0:1] == marks)
            placed = dot(picks, blocks)
            if part == 0:
                total_ref[rows, :] = placed
            else:
                total_ref[rows, :] += placed

    cache_ref[...] = total_ref[:CAP, :].astype(jnp.bfloat16)

    @pl.loop(1, n_batch)
    def _(step):
        copy(step).wait_send()

    for which in range(6):
        ring(which).wait_send()
    for which in range(7):
        share(which).wait_send()
    for step in range(1, 8):
        id_copy(step).wait_send()
    wp_swap().wait_send()
    for dx in range(1, 4):
        wp_x(dx).wait_send()
        for dy in range(1, 4):
            wp_y(dx, dy).wait_send()

    @pl.loop(0, 5)
    def _(part):
        for dx in range(1, 4):
            a_copy(dx, part).wait_send()
        for dx in range(4):
            a_share(dx, part).wait_send()
        s_copy(part).wait_send()


def encode(*arrays):
    vmem = pl.BlockSpec(memory_space=pltpu.VMEM)
    n_batch = lax.axis_size("batch")
    dma = pltpu.SemaphoreType.DMA
    bf16, f32 = jnp.bfloat16, jnp.float32
    return pl.pallas_call(
        encode_kernel,
        out_shape=jax.ShapeDtypeStruct((CAP, GROUP), bf16),
        in_specs=[vmem] * len(arrays),
        out_specs=vmem,
        scratch_shapes=[
            pltpu.VMEM((GROUP, GROUP), bf16),
            pltpu.VMEM((128, 128), f32),
            pltpu.VMEM((128, 128), f32),
            pltpu.VMEM((160, 128), f32),
            pltpu.VMEM((160, 128), jnp.int32),
            pltpu.VMEM((8, GROUP), f32),
            pltpu.VMEM((ROWS, 128), f32),
            pltpu.VMEM((n_batch, SLOTS, GROUP), bf16),
            pltpu.VMEM((n_batch, SLOTS, GROUP), bf16),
            pltpu.VMEM((ROWS, GROUP), f32),
            dma((n_batch,)), dma((n_batch,)),
            pltpu.VMEM((2560, WIDTH), bf16),
            pltpu.VMEM((TALL, WIDTH), bf16),
            pltpu.VMEM((480, 128), f32),
            pltpu.VMEM((160, 2560), bf16),
            pltpu.VMEM((320, TALL), bf16),
            pltpu.VMEM((512, 512), bf16),
            pltpu.VMEM((8, 128), jnp.int32),
            pltpu.VMEM((8, 8, 128), jnp.int32),
            pltpu.VMEM((8, 2560), f32),
            pltpu.VMEM((TALL, 128), f32),
            pltpu.VMEM((160, 2560), bf16),
            pltpu.VMEM((4, 160, GROUP), bf16),
            pltpu.VMEM((WIDTH, GROUP), bf16),
            pltpu.VMEM((WIDTH, GROUP), bf16),
            pltpu.VMEM((GROUP, GROUP), f32),
            pltpu.VMEM((GROUP, 128), f32),
            pltpu.VMEM((GROUP, 128), f32),
            dma((6,)), dma((6,)), dma((7,)), dma((7,)), dma((8,)), dma((8,)),
            dma((2,)), dma((2, 3)), dma((2, 9)),
            dma((3, 5)), dma((3, 5)), dma((4, 5)), dma((4, 5)), dma((2, 5)),
        ],
        compiler_params=pltpu.CompilerParams(
            collective_id=0, has_side_effects=True, vmem_limit_bytes=56 * 1024 * 1024
        ),
    )(*arrays)


def shards(
    patches, window_ids, norm_gain, w_qkv, b_qkv, w_proj, b_proj, merge_gain, token_lists, req_owner, req_counts
):
    return encode(
        patches[0],
        window_ids,
        norm_gain.reshape(10, 128),
        jnp.transpose(w_qkv, (0, 2, 1)).reshape(480, WIDTH),
        b_qkv,
        w_proj,
        b_proj.reshape(10, 128),
        merge_gain.reshape(10, 128),
        token_lists.reshape(160, 128),
        req_owner[None],
        req_counts[None],
    )[None]


def solution(mesh):
    return jax.shard_map(
        shards,
        mesh=mesh,
        in_specs=(
            P("batch", "seq", None),
            P("batch", "seq"),
            P(),
            P(None, None, "seq"),
            P(),
            P("seq", None),
            P(),
            P(),
            P(),
            P(),
            P(),
        ),
        out_specs=P("batch", None, "seq"),
        check_vma=False,
    )
```

```python
import math

import jax
import jax.numpy as jnp
from jax import lax
from jax.experimental import pallas as pl
from jax.experimental.pallas import tpu as pltpu
from jax.sharding import PartitionSpec as P

REQS = 4
WIDTH = 1280
TALL = 2688
SCALE = math.log2(math.e) / math.sqrt(80)
SLOTS = 40
GROUP = 640
MOST = 319
CAP = 1276
ROWS = 1280
PER = 8


def dot(left, right, dims=((1,), (0,))):
    return lax.dot_general(left, right, (dims, ((), ())), preferred_element_type=jnp.float32)


def iota(shape, axis):
    return lax.broadcasted_iota(jnp.int32, shape, axis)


def onehot(condition):
    return jnp.where(condition, 1.0, 0.0).astype(jnp.bfloat16)


def lanes_of(ref, first, count):
    return jnp.concatenate([ref[pl.ds(first + at, 1), :] for at in range(count)], axis=1)


def tables(tok_ref, owner_ref, count_ref, batch, steps, jumps, owners, dests, slot, source):
    f32 = jnp.float32
    me = batch.astype(f32)
    counts = count_ref[...].astype(f32)
    owner = owner_ref[...].astype(f32)

    def flip(row):
        return jnp.transpose(jnp.broadcast_to(row, (128, 128)))

    lower = iota((128, 128), 0) < iota((128, 128), 1)
    owner_down = flip(owner)
    starts = jnp.sum(jnp.where(lower, flip(counts), 0.0), axis=0, keepdims=True)
    ranks = jnp.sum(jnp.where(lower & (owner_down == owner), 1.0, 0.0), axis=0, keepdims=True)
    steps[...] = flip(starts)
    previous = jnp.where(iota((128, 128), 0) == 0, 0.0, pltpu.roll(owner_down, 1, 0))
    jumps[...] = owner_down - previous
    places = (iota((160, 128), 0) * 128 + iota((160, 128), 1)).astype(f32)

    def jump(request, held):
        return held + jnp.where(places >= steps[pl.ds(request, 1), :], jumps[pl.ds(request, 1), :], 0.0)

    owners[...] = lax.fori_loop(0, 128, jump, jnp.zeros((160, 128), f32), unroll=4)
    dest = jnp.zeros((160, 128), f32)
    for rank in range(REQS):
        chosen = (owner == me) & (ranks == rank)
        start = jnp.sum(jnp.where(chosen, starts, 0.0), axis=1, keepdims=True)
        count = jnp.sum(jnp.where(chosen, counts, 0.0), axis=1, keepdims=True)
        within = (places >= start) & (places < start + count)
        dest = dest + jnp.where(within, places - start + (MOST * rank + 1), 0.0)
    dests[...] = dest.astype(jnp.int32) - 1

    def gather(part, sums):
        rows = pl.ds(pl.multiple_of(part * 8, 8), 8)
        token = tok_ref[rows, :]
        local = token - batch * GROUP
        dest = dests[rows, :]
        owner = owners[rows, :] + 1.0
        high = (token >> 7).astype(f32) + 1.0
        low = (token & 127).astype(f32)
        down, short = iota((128, 128), 0), iota((16, 128), 0)
        group_left, group_right, own_left, own_right = [], [], [], []
        for at in range(8):
            row = slice(at, at + 1)
            group_left.append(onehot(down == (local[row] & 127)))
            group_right.append(jnp.where(short == (local[row] >> 7), owner[row], 0.0).astype(jnp.bfloat16))
            own_left.append(onehot(down == (dest[row] & 127)))
            mine = short == (dest[row] >> 7)
            own_right.append(
                jnp.concatenate([jnp.where(mine, high[row], 0.0), jnp.where(mine, low[row], 0.0)], axis=0).astype(
                    jnp.bfloat16
                )
            )
        first = dot(jnp.concatenate(group_left, axis=1), jnp.concatenate(group_right, axis=1), ((1,), (1,)))
        second = dot(jnp.concatenate(own_left, axis=1), jnp.concatenate(own_right, axis=1), ((1,), (1,)))
        return sums[0] + first, sums[1] + second

    owner_cols, token_cols = lax.fori_loop(
        0, 20, gather, (jnp.zeros((128, 16), f32), jnp.zeros((128, 32), f32))
    )
    unit = onehot(iota((128, 128), 0) == iota((128, 128), 1))
    owner_rows = dot(owner_cols.astype(jnp.bfloat16), unit, ((0,), (0,)))
    token_rows = dot(token_cols.astype(jnp.bfloat16), unit, ((0,), (0,)))

    owner_row = jnp.concatenate([owner_rows[at : at + 1] for at in range(5)], axis=1)
    before = jnp.zeros((1, GROUP), f32)
    for at in range(5):
        same = (owner_cols[:, at : at + 1] == owner_row) & (
            iota((128, GROUP), 0) + at * 128 < iota((128, GROUP), 1)
        )
        before = before + jnp.sum(jnp.where(same, 1.0, 0.0), axis=0, keepdims=True)
    slot[...] = jnp.broadcast_to((owner_row - 1.0) * SLOTS + before, (8, GROUP))

    token_row = jnp.concatenate(
        [(token_rows[at : at + 1] - 1.0) * 128 + token_rows[at + 16 : at + 17] for at in range(10)], axis=1
    )
    for at in range(10):
        high = token_cols[:, at : at + 1] - 1.0
        token = high * 128 + token_cols[:, at + 16 : at + 17]
        group = jnp.floor((high + 0.5) * 0.2)
        earlier = jnp.where((token_row < token) & (token_row >= group * GROUP), 1.0, 0.0)
        taken = jnp.sum(earlier, axis=1, keepdims=True)
        found = jnp.where(high >= 0.0, group * SLOTS + taken, -1.0)
        source[at * 128 : at * 128 + 128, :] = jnp.broadcast_to(found, (128, 128))


def encode_kernel(
    patch_ref, ids_ref, gain_ref, w_ref, b_ref, wproj_ref, bproj_ref, merge_ref, tok_ref, owner_ref, count_ref,
    cache_ref, merged_ref, steps, jumps, owners, dests, slot, source, packed, landed, total_ref, send_sem, land_sem,
    raw, xn, wt, wk, bias, bias_col, bias_row, q, k, v, perm, id_send, id_land, id_row, id_col, attn, pieces, mixed, wp, resid,
    sums_out, sums_in, x_send, x_land, d_send, d_land, i_send, i_land, ws_sem, wx_sem, wy_sem,
    a_send, a_land, f_send, f_land, s_sem, l_sem,
):
    place = lax.axis_index("seq")
    batch = lax.axis_index("batch")
    n_batch = lax.axis_size("batch")
    x, core = place // 2, place % 2
    row_y = batch % 4
    column = batch - row_y
    sibling = place + 1 - 2 * core
    right = lax.rem(x + 1, 4) * 2 + core
    left = lax.rem(x + 3, 4) * 2 + core
    own_rows = pl.ds(pl.multiple_of(place * 320, 32), 320)
    own_load = pltpu.make_async_copy(patch_ref, raw.at[own_rows, :], l_sem.at[0])
    w_load = pltpu.make_async_copy(w_ref, wt, l_sem.at[1])
    own_load.start()
    w_load.start()
    barrier = pltpu.get_barrier_semaphore()

    for step in range(1, 8):
        pl.semaphore_signal(barrier, inc=1, device_id={"seq": lax.rem(place + step, 8)})

    @pl.loop(1, n_batch)
    def _(step):
        pl.semaphore_signal(barrier, inc=1, device_id={"batch": lax.rem(batch + step, n_batch)})

    pl.semaphore_wait(barrier, 7 + n_batch - 1)

    def rows_of(chip, half=None):
        start = lax.rem(chip, 4) * 640 + core * 320
        if half is None:
            return pl.ds(pl.multiple_of(start, 32), 320)
        return pl.ds(pl.multiple_of(start + half * 160, 32), 160)

    def remote(src, dst, send, land, **device):
        return pltpu.make_async_remote_copy(
            src_ref=src, dst_ref=dst, send_sem=send, recv_sem=land, device_id=device
        )

    def ring(which):
        half = (0, 1, 1, 0, 0, 1)[which]
        target = (right, left, right, left, right, left)[which]
        if which < 4:
            src = patch_ref.at[pl.ds(half * 160, 160), :]
            dst = raw.at[rows_of(x, half), :]
        else:
            rows = rows_of(x + 3 if which == 4 else x + 1, half)
            src, dst = raw.at[rows, :], raw.at[rows, :]
        return remote(src, dst, x_send.at[which], x_land.at[which], seq=target)

    def share(which):
        if which == 6:
            return remote(patch_ref, raw.at[rows_of(x), :], d_send.at[6], d_land.at[6], seq=sibling)
        chip = x + (3, 1, 3, 1, 2, 2)[which]
        rows = rows_of(chip, (0, 1, 1, 0, 0, 1)[which])
        return remote(raw.at[rows, :], raw.at[rows, :], d_send.at[which], d_land.at[which], seq=sibling)

    def id_copy(step):
        return remote(
            id_send, id_land.at[place], i_send.at[step], i_land.at[step], seq=lax.rem(place + step, 8)
        )

    own_wrows = pl.ds(pl.multiple_of(place * 160, 32), 160)

    def wp_swap():
        columns = pl.ds(pl.multiple_of((1 - core) * 640, 128), 640)
        return remote(wproj_ref.at[:, columns], wp.at[own_wrows, :], ws_sem.at[0], ws_sem.at[1], seq=sibling)

    def wp_part(chip):
        return pl.ds(pl.multiple_of(lax.rem(chip, 4) * 320 + row_y * 80, 16), 80)

    def wp_x(dx):
        rows = wp_part(x)
        target = lax.rem(x + dx, 4) * 2 + core
        return remote(wp.at[rows, :], wp.at[rows, :], wx_sem.at[0, dx - 1], wx_sem.at[1, dx - 1], seq=target)

    def wp_y(dx, dy):
        rows = wp_part(x + 4 - dx)
        index = (dx - 1) * 3 + dy - 1
        return remote(
            wp.at[rows, :], wp.at[rows, :], wy_sem.at[0, index], wy_sem.at[1, index],
            batch=column + lax.rem(row_y + dy, 4),
        )

    id_send[...] = jnp.zeros_like(id_send)
    id_send[0:1, 0:80] = ids_ref[...]
    share(6).start()
    ring(0).start()
    ring(1).start()
    for step in range(1, 8):
        id_copy(step).start()
    wp_swap().start()
    ring(2).start()
    ring(3).start()

    wp[own_wrows, :] = wproj_ref[:, pl.ds(pl.multiple_of(core * 640, 128), 640)]
    id_land[place] = id_send[...]
    xn[0:64, :] = jnp.zeros((64, WIDTH), jnp.bfloat16)
    xn[TALL - 64 : TALL, :] = jnp.zeros((64, WIDTH), jnp.bfloat16)
    for which in range(3):
        rows = pl.ds(which * 160, 160)
        lanes = iota((160, WIDTH), 1) == iota((160, WIDTH), 0) + place * 160
        picked = jnp.sum(jnp.where(lanes, b_ref[which : which + 1, :], 0.0), axis=1, keepdims=True)
        bias[rows, :] = jnp.broadcast_to(picked, (160, 128))
    bias_col[...] = jnp.zeros_like(bias_col)
    for head in range(2):
        bias_col[head * 128 : head * 128 + 80, :] = bias[160 + head * 80 : 240 + head * 80, :]
        flipped = jnp.transpose(bias_col[head * 128 : head * 128 + 128, :])
        bias_row[:, head * 128 : head * 128 + 128] = flipped[0:8, :]
    inner = iota((512, 512), 1)
    perm[...] = onehot(iota((512, 512), 0) == (inner & 127) * 4 + (inner >> 7))

    def project(first, xrow, columns, out):
        product = dot(wt[first : first + 160, :], xn[xrow, :], ((1,), (1,)))
        out[:, columns] = (product + bias[first : first + 160, 0:1]).astype(jnp.bfloat16)

    def project_keys(rows):
        product = dot(xn[rows, :], wk[...], ((1,), (1,)))
        k[rows, :] = (product + bias_row[0:1, :]).astype(jnp.bfloat16)

    def attend(block):
        own = pl.ds(pl.multiple_of(block * 128, 128), 128)
        band = pl.ds(pl.multiple_of(block * 128, 128), 256)
        matches = id_col[band, :] == id_row[0:1, own]
        for head in range(2):
            feats = slice(head * 80, head * 80 + 80)
            scores = dot(k[band, head * 128 : head * 128 + 80], q[feats, own])
            scores = jnp.where(matches, scores, -1e30)
            peak = jnp.max(scores, axis=0, keepdims=True)
            weights = jnp.exp2((scores - peak) * SCALE)
            total = jnp.sum(weights, axis=0, keepdims=True)
            out = dot(v[feats, band], weights.astype(jnp.bfloat16))
            attn[feats, own] = (out * (1.0 / total)).astype(jnp.bfloat16)

    def normalise(chip, halves):
        gain = lanes_of(gain_ref, 0, 10)
        for at in range(2):
            for half in halves:
                first = lax.rem(chip, 4) * 640 + at * 320 + half * 160

                @pl.loop(0, 10, unroll=2)
                def _(tile):
                    start = pl.multiple_of(first + tile * 16, 16)
                    rows = raw[pl.ds(start, 16), :].astype(jnp.float32)
                    level = lax.rsqrt(jnp.mean(rows * rows, axis=1, keepdims=True) + 1e-06)
                    xn[pl.ds(pl.multiple_of(start + 64, 16), 16), :] = (rows * level * gain).astype(jnp.bfloat16)

    def take_chip(chip):
        chip = lax.rem(chip, 4)
        base = chip * 640
        project(0, pl.ds(pl.multiple_of(base + 64, 64), 640), pl.ds(pl.multiple_of(base, 128), 640), q)
        wide = pl.ds(pl.multiple_of(base + 128, 128), 512)
        project_keys(wide)
        project(320, wide, wide, v)

        units = jnp.concatenate([id_land[chip * 2, 0:1, :], id_land[chip * 2 + 1, 0:1, :]], axis=1)
        units = units.astype(jnp.float32).astype(jnp.bfloat16)
        spread = iota((640, 256), 0)
        spread = onehot(jnp.where(spread < 320, spread >> 2, ((spread - 320) >> 2) + 128) == iota((640, 256), 1))
        id_row[:, pl.ds(pl.multiple_of(base, 128), 640)] = dot(
            jnp.broadcast_to(units, (8, 256)), spread, ((1,), (1,))
        )
        id_col[pl.ds(pl.multiple_of(base + 64, 64), 640), :] = dot(
            spread, jnp.broadcast_to(units, (128, 256)), ((1,), (1,))
        )
        for tile in range(1, 4):
            attend(chip * 5 + tile)

    def take_edge(edge):
        columns = pl.ds(pl.multiple_of(edge * 640, 128), 128)
        project_keys(columns)
        project(320, columns, columns, v)

        @pl.when(edge > 0)
        def _():
            attend(edge * 5 - 1)

        @pl.when(edge < 4)
        def _():
            attend(edge * 5)

    def chunk_of(part):
        return pl.ds(pl.multiple_of(part * 128, 128), 128)

    def feats_of(chip, at):
        return pl.ds(pl.multiple_of(lax.rem(chip, 4) * 320 + at * 160, 32), 160)

    def a_copy(dx, part):
        chip = lax.rem(x + dx, 4)
        return remote(
            pieces.at[chip, :, chunk_of(part)],
            mixed.at[feats_of(x, core), chunk_of(part)],
            a_send.at[dx - 1, part],
            a_land.at[dx - 1, part],
            seq=chip * 2 + core,
        )

    def a_share(dx, part):
        block = mixed.at[feats_of(x + 4 - dx, core), chunk_of(part)]
        return remote(block, block, f_send.at[dx, part], f_land.at[dx, part], seq=sibling)

    def late_chip(chip):
        return lax.rem(chip + 2, 4)

    def early(chip, at):
        return lax.rem(late_chip(chip) + 2 + at, 5)

    def sort_chunk(part):
        chunk = attn[:, pl.ds(pl.multiple_of(part * 512, 128), 512)]
        sorted_rows = dot(chunk, perm[...]).astype(jnp.bfloat16)
        for dest in range(4):
            pieces[dest, :, chunk_of(part)] = sorted_rows[:, dest * 128 : dest * 128 + 128]
        mixed[feats_of(x, core), chunk_of(part)] = pieces[x, :, chunk_of(part)]

    def send_chunk(part):
        for dx in (2, 1, 3):
            a_copy(dx, part).start()
        a_share(0, part).start()

    id_col[0:64, :] = jnp.full((64, 128), -1.0, jnp.float32)
    id_col[TALL - 64 : TALL, :] = jnp.full((64, 128), -1.0, jnp.float32)
    w_load.wait()
    wk[...] = jnp.zeros_like(wk)
    for head in range(2):
        wk[head * 128 : head * 128 + 80, :] = wt[160 + head * 80 : 240 + head * 80, :]
    wp_swap().wait_recv()
    for dx in range(1, 4):
        wp_x(dx).start()
    tables(tok_ref, owner_ref, count_ref, batch, steps, jumps, owners, dests, slot, source)
    own_load.wait()
    for step in range(1, 8):
        id_copy(step).wait_recv()
    share(6).wait_recv()
    normalise(x, (0, 1))
    take_chip(x)
    for which in (0, 1):
        ring(which).wait_recv()
        ring(which + 4).start()
        share(which).start()
    for dx in range(1, 4):
        wp_x(dx).wait_recv()
        for dy in range(1, 4):
            wp_y(dx, dy).start()
    share(0).wait_recv()
    share(1).wait_recv()
    normalise(x + 3, (0,))
    normalise(x + 1, (1,))
    for which in (2, 3):
        ring(which).wait_recv()
        share(which).start()
    share(2).wait_recv()
    normalise(x + 3, (1,))
    take_chip(x + 3)
    share(3).wait_recv()
    normalise(x + 1, (0,))
    take_chip(x + 1)

    @pl.loop(0, 3)
    def _(at):
        take_edge(early(x, at))

    @pl.loop(0, 3)
    def _(at):
        sort_chunk(early(x, at))

    for which in (4, 5):
        ring(which).wait_recv()
        share(which).start()

    @pl.loop(0, 3)
    def _(at):
        send_chunk(early(x, at))

    for which in (4, 5):
        share(which).wait_recv()
    normalise(x + 2, (0, 1))
    take_chip(x + 2)

    @pl.loop(0, 2)
    def _(at):
        take_edge(late_chip(x) + at)

    @pl.loop(0, 2)
    def _(at):
        sort_chunk(late_chip(x) + at)
        send_chunk(late_chip(x) + at)

    def pass_on(dx, part):
        a_copy(dx, part).wait_recv()
        a_share(dx, part).start()

    @pl.loop(0, 3)
    def _(at):
        for dx in (1, 3, 2):
            pass_on(dx, early(x + 4 - dx, at))

    half = pl.ds(pl.multiple_of(core * 640, 128), 640)
    pick = onehot(iota((128, 512), 1) == iota((128, 512), 0) * 4 + x)

    @pl.loop(0, 5)
    def _(part):
        rows = raw[pl.ds(pl.multiple_of(part * 512, 128), 512), half]
        resid[chunk_of(part), :] = dot(pick, rows) + lanes_of(bproj_ref, core * 5, 5)

    @pl.loop(0, 2)
    def _(at):
        for dx in (1, 3, 2):
            pass_on(dx, late_chip(x + 4 - dx) + at)

    for dx in range(1, 4):
        for dy in range(1, 4):
            wp_y(dx, dy).wait_recv()

    def s_copy(part):
        return remote(
            sums_out.at[chunk_of(part), :], sums_in.at[chunk_of(part), :], s_sem.at[0, part], s_sem.at[1, part],
            seq=sibling,
        )

    @pl.loop(0, 5)
    def _(part):
        for dx in (0, 1, 3, 2):
            a_share(dx, part).wait_recv()
        rows = resid[chunk_of(part), :] + dot(mixed[:, chunk_of(part)], wp[...], ((0,), (0,)))
        resid[chunk_of(part), :] = rows
        total = jnp.sum(rows * rows, axis=1, keepdims=True)
        sums_out[chunk_of(part), :] = jnp.broadcast_to(total, (128, 128))
        s_copy(part).start()

    @pl.loop(0, 5)
    def _(part):
        s_copy(part).wait_recv()
        total = sums_out[chunk_of(part), 0:1] + sums_in[chunk_of(part), 0:1]
        level = lax.rsqrt(total * (1.0 / WIDTH) + 1e-06)
        merged_ref[chunk_of(part), :] = (resid[chunk_of(part), :] * level * lanes_of(merge_ref, core * 5, 5)).astype(jnp.bfloat16)

    def copy(step):
        return pltpu.make_async_remote_copy(
            src_ref=packed.at[step],
            dst_ref=landed.at[step],
            send_sem=send_sem.at[step],
            recv_sem=land_sem.at[step],
            device_id={"batch": lax.rem(batch + step, n_batch)},
        )

    @pl.loop(0, n_batch // PER)
    def _(part):
        wanted = iota((PER * SLOTS, GROUP), 0) + (batch + part * PER) * SLOTS
        wanted = jnp.where(wanted >= ROWS, wanted - ROWS, wanted).astype(jnp.float32)
        rows = dot(onehot(slot[0:1, :] == wanted), merged_ref[...]).astype(jnp.bfloat16)
        for inner in range(PER):
            packed[part * PER + inner] = rows[inner * SLOTS : inner * SLOTS + SLOTS]
        for inner in range(PER):
            step = part * PER + inner

            @pl.when(step > 0)
            def _():
                copy(step).start()

    landed[0] = packed[0]

    step = 0
    for count in (12, 12, 6, 2):
        marks = []
        blocks = []
        for _ in range(count):
            if step > 0:
                copy(step).wait_recv()
            blocks.append(landed[step])
            group = lax.rem(batch - step + n_batch, n_batch)
            marks.append((iota((1, SLOTS), 1) + group * SLOTS).astype(jnp.float32))
            step += 1
        marks = jnp.concatenate(marks, axis=1)
        blocks = jnp.concatenate(blocks, axis=0)
        for first in (0, GROUP):
            rows = slice(first, first + GROUP)
            placed = dot(onehot(source[rows, 0:1] == marks), blocks)
            if step > count:
                placed += total_ref[rows, :]
            if step < 32:
                total_ref[rows, :] = placed
            else:
                last = min(first + GROUP, CAP)
                cache_ref[first:last, :] = placed[: last - first].astype(jnp.bfloat16)

    @pl.loop(1, n_batch)
    def _(step):
        copy(step).wait_send()

    for which in range(6):
        ring(which).wait_send()
    for which in range(7):
        share(which).wait_send()
    for step in range(1, 8):
        id_copy(step).wait_send()
    wp_swap().wait_send()
    for dx in range(1, 4):
        wp_x(dx).wait_send()
        for dy in range(1, 4):
            wp_y(dx, dy).wait_send()

    @pl.loop(0, 5)
    def _(part):
        for dx in range(1, 4):
            a_copy(dx, part).wait_send()
        for dx in range(4):
            a_share(dx, part).wait_send()
        s_copy(part).wait_send()


def encode(*arrays):
    vmem = pl.BlockSpec(memory_space=pltpu.VMEM)
    hbm = pl.BlockSpec(memory_space=pl.ANY)
    n_batch = lax.axis_size("batch")
    dma = pltpu.SemaphoreType.DMA
    bf16, f32 = jnp.bfloat16, jnp.float32
    return pl.pallas_call(
        encode_kernel,
        out_shape=jax.ShapeDtypeStruct((CAP, GROUP), bf16),
        in_specs=[hbm, vmem, vmem, hbm] + [vmem] * (len(arrays) - 4),
        out_specs=vmem,
        scratch_shapes=[
            pltpu.VMEM((GROUP, GROUP), bf16),
            pltpu.VMEM((128, 128), f32),
            pltpu.VMEM((128, 128), f32),
            pltpu.VMEM((160, 128), f32),
            pltpu.VMEM((160, 128), jnp.int32),
            pltpu.VMEM((8, GROUP), f32),
            pltpu.VMEM((ROWS, 128), f32),
            pltpu.VMEM((n_batch, SLOTS, GROUP), bf16),
            pltpu.VMEM((n_batch, SLOTS, GROUP), bf16),
            pltpu.VMEM((ROWS, GROUP), f32),
            dma((n_batch,)), dma((n_batch,)),
            pltpu.VMEM((2560, WIDTH), bf16),
            pltpu.VMEM((TALL, WIDTH), bf16),
            pltpu.VMEM((480, WIDTH), bf16),
            pltpu.VMEM((256, WIDTH), bf16),
            pltpu.VMEM((480, 128), f32),
            pltpu.VMEM((256, 128), f32),
            pltpu.VMEM((8, 256), f32),
            pltpu.VMEM((160, 2560), bf16),
            pltpu.VMEM((TALL, 256), bf16),
            pltpu.VMEM((160, TALL), bf16),
            pltpu.VMEM((512, 512), bf16),
            pltpu.VMEM((8, 128), jnp.int32),
            pltpu.VMEM((8, 8, 128), jnp.int32),
            pltpu.VMEM((8, 2560), f32),
            pltpu.VMEM((TALL, 128), f32),
            pltpu.VMEM((160, 2560), bf16),
            pltpu.VMEM((4, 160, GROUP), bf16),
            pltpu.VMEM((WIDTH, GROUP), bf16),
            pltpu.VMEM((WIDTH, GROUP), bf16),
            pltpu.VMEM((GROUP, GROUP), f32),
            pltpu.VMEM((GROUP, 128), f32),
            pltpu.VMEM((GROUP, 128), f32),
            dma((6,)), dma((6,)), dma((7,)), dma((7,)), dma((8,)), dma((8,)),
            dma((2,)), dma((2, 3)), dma((2, 9)),
            dma((3, 5)), dma((3, 5)), dma((4, 5)), dma((4, 5)), dma((2, 5)), dma((2,)),
        ],
        compiler_params=pltpu.CompilerParams(
            collective_id=0, has_side_effects=True, vmem_limit_bytes=56 * 1024 * 1024
        ),
    )(*arrays)


def shards(
    patches, window_ids, norm_gain, w_qkv, b_qkv, w_proj, b_proj, merge_gain, token_lists, req_owner, req_counts
):
    return encode(
        patches[0],
        window_ids,
        norm_gain.reshape(10, 128),
        jnp.transpose(w_qkv, (0, 2, 1)).reshape(480, WIDTH),
        b_qkv,
        w_proj,
        b_proj.reshape(10, 128),
        merge_gain.reshape(10, 128),
        token_lists.reshape(160, 128),
        req_owner[None],
        req_counts[None],
    )[None]


def solution(mesh):
    return jax.shard_map(
        shards,
        mesh=mesh,
        in_specs=(
            P("batch", "seq", None),
            P("batch", "seq"),
            P(),
            P(None, None, "seq"),
            P(),
            P("seq", None),
            P(),
            P(),
            P(),
            P(),
            P(),
        ),
        out_specs=P("batch", None, "seq"),
        check_vma=False,
    )
```

```python
import math

import jax
import jax.numpy as jnp
from jax import lax
from jax.experimental import pallas as pl
from jax.experimental.pallas import tpu as pltpu
from jax.sharding import PartitionSpec as P

REQS = 4
WIDTH = 1280
TALL = 2688
SCALE = math.log2(math.e) / math.sqrt(80)
SLOTS = 40
GROUP = 640
MOST = 319
CAP = 1276
ROWS = 1280
PER = 8


def dot(left, right, dims=((1,), (0,))):
    return lax.dot_general(left, right, (dims, ((), ())), preferred_element_type=jnp.float32)


def iota(shape, axis):
    return lax.broadcasted_iota(jnp.int32, shape, axis)


def onehot(condition):
    return jnp.where(condition, 1.0, 0.0).astype(jnp.bfloat16)


def lanes_of(ref, first, count):
    return jnp.concatenate([ref[pl.ds(first + at, 1), :] for at in range(count)], axis=1)


def tables(tok_ref, owner_ref, count_ref, batch, steps, jumps, owners, dests, slot, source):
    f32 = jnp.float32
    me = batch.astype(f32)
    counts = count_ref[...].astype(f32)
    owner = owner_ref[...].astype(f32)

    def flip(row):
        return jnp.transpose(jnp.broadcast_to(row, (128, 128)))

    lower = iota((128, 128), 0) < iota((128, 128), 1)
    owner_down = flip(owner)
    starts = jnp.sum(jnp.where(lower, flip(counts), 0.0), axis=0, keepdims=True)
    ranks = jnp.sum(jnp.where(lower & (owner_down == owner), 1.0, 0.0), axis=0, keepdims=True)
    steps[...] = flip(starts)
    previous = jnp.where(iota((128, 128), 0) == 0, 0.0, pltpu.roll(owner_down, 1, 0))
    jumps[...] = owner_down - previous
    places = (iota((160, 128), 0) * 128 + iota((160, 128), 1)).astype(f32)

    def jump(request, held):
        return held + jnp.where(places >= steps[pl.ds(request, 1), :], jumps[pl.ds(request, 1), :], 0.0)

    owners[...] = lax.fori_loop(0, 128, jump, jnp.zeros((160, 128), f32), unroll=4)
    dest = jnp.zeros((160, 128), f32)
    for rank in range(REQS):
        chosen = (owner == me) & (ranks == rank)
        start = jnp.sum(jnp.where(chosen, starts, 0.0), axis=1, keepdims=True)
        count = jnp.sum(jnp.where(chosen, counts, 0.0), axis=1, keepdims=True)
        within = (places >= start) & (places < start + count)
        dest = dest + jnp.where(within, places - start + (MOST * rank + 1), 0.0)
    dests[...] = dest.astype(jnp.int32) - 1

    def gather(part, sums):
        rows = pl.ds(pl.multiple_of(part * 8, 8), 8)
        token = tok_ref[rows, :]
        local = token - batch * GROUP
        dest = dests[rows, :]
        owner = owners[rows, :] + 1.0
        high = (token >> 7).astype(f32) + 1.0
        low = (token & 127).astype(f32)
        down, short = iota((128, 128), 0), iota((16, 128), 0)
        group_left, group_right, own_left, own_right = [], [], [], []
        for at in range(8):
            row = slice(at, at + 1)
            group_left.append(onehot(down == (local[row] & 127)))
            group_right.append(jnp.where(short == (local[row] >> 7), owner[row], 0.0).astype(jnp.bfloat16))
            own_left.append(onehot(down == (dest[row] & 127)))
            mine = short == (dest[row] >> 7)
            own_right.append(
                jnp.concatenate([jnp.where(mine, high[row], 0.0), jnp.where(mine, low[row], 0.0)], axis=0).astype(
                    jnp.bfloat16
                )
            )
        first = dot(jnp.concatenate(group_left, axis=1), jnp.concatenate(group_right, axis=1), ((1,), (1,)))
        second = dot(jnp.concatenate(own_left, axis=1), jnp.concatenate(own_right, axis=1), ((1,), (1,)))
        return sums[0] + first, sums[1] + second

    owner_cols, token_cols = lax.fori_loop(
        0, 20, gather, (jnp.zeros((128, 16), f32), jnp.zeros((128, 32), f32))
    )
    unit = onehot(iota((128, 128), 0) == iota((128, 128), 1))
    owner_rows = dot(owner_cols.astype(jnp.bfloat16), unit, ((0,), (0,)))
    token_rows = dot(token_cols.astype(jnp.bfloat16), unit, ((0,), (0,)))

    owner_row = jnp.concatenate([owner_rows[at : at + 1] for at in range(5)], axis=1)
    before = jnp.zeros((1, GROUP), f32)
    for at in range(5):
        same = (owner_cols[:, at : at + 1] == owner_row) & (
            iota((128, GROUP), 0) + at * 128 < iota((128, GROUP), 1)
        )
        before = before + jnp.sum(jnp.where(same, 1.0, 0.0), axis=0, keepdims=True)
    slot[...] = jnp.broadcast_to((owner_row - 1.0) * SLOTS + before, (8, GROUP))

    token_row = jnp.concatenate(
        [(token_rows[at : at + 1] - 1.0) * 128 + token_rows[at + 16 : at + 17] for at in range(10)], axis=1
    )
    for at in range(10):
        high = token_cols[:, at : at + 1] - 1.0
        token = high * 128 + token_cols[:, at + 16 : at + 17]
        group = jnp.floor((high + 0.5) * 0.2)
        earlier = jnp.where((token_row < token) & (token_row >= group * GROUP), 1.0, 0.0)
        taken = jnp.sum(earlier, axis=1, keepdims=True)
        found = jnp.where(high >= 0.0, group * SLOTS + taken, -1.0)
        source[at * 128 : at * 128 + 128, :] = jnp.broadcast_to(found, (128, 128))


def encode_kernel(
    patch_ref, ids_ref, gain_ref, w_ref, b_ref, wproj_ref, bproj_ref, merge_ref, tok_ref, owner_ref, count_ref,
    cache_ref, merged_ref, steps, jumps, owners, dests, slot, source, packed, landed, total_ref, send_sem, land_sem,
    raw, xn, wt, wk, bias, bias_col, bias_row, q, k, v, perm, id_send, id_land, id_row, id_col, attn, pieces, mixed, wp, resid,
    sums_out, sums_in, x_send, x_land, d_send, d_land, i_send, i_land, ws_sem, wx_sem, wy_sem,
    a_send, a_land, f_send, f_land, s_sem, l_sem,
):
    place = lax.axis_index("seq")
    batch = lax.axis_index("batch")
    n_batch = lax.axis_size("batch")
    x, core = place // 2, place % 2
    row_y = batch % 4
    column = batch - row_y
    sibling = place + 1 - 2 * core
    right = lax.rem(x + 1, 4) * 2 + core
    left = lax.rem(x + 3, 4) * 2 + core
    own_rows = pl.ds(pl.multiple_of(place * 320, 32), 320)
    own_load = pltpu.make_async_copy(patch_ref, raw.at[own_rows, :], l_sem.at[0])
    w_load = pltpu.make_async_copy(w_ref, wt, l_sem.at[1])
    own_load.start()
    w_load.start()
    barrier = pltpu.get_barrier_semaphore()

    for step in range(1, 8):
        pl.semaphore_signal(barrier, inc=1, device_id={"seq": lax.rem(place + step, 8)})

    @pl.loop(1, n_batch)
    def _(step):
        pl.semaphore_signal(barrier, inc=1, device_id={"batch": lax.rem(batch + step, n_batch)})

    pl.semaphore_wait(barrier, 7 + n_batch - 1)

    def rows_of(chip, half=None):
        start = lax.rem(chip, 4) * 640 + core * 320
        if half is None:
            return pl.ds(pl.multiple_of(start, 32), 320)
        return pl.ds(pl.multiple_of(start + half * 160, 32), 160)

    def remote(src, dst, send, land, **device):
        return pltpu.make_async_remote_copy(
            src_ref=src, dst_ref=dst, send_sem=send, recv_sem=land, device_id=device
        )

    def ring(which):
        half = (0, 1, 1, 0, 0, 1)[which]
        target = (right, left, right, left, right, left)[which]
        if which < 4:
            src = patch_ref.at[pl.ds(half * 160, 160), :]
            dst = raw.at[rows_of(x, half), :]
        else:
            rows = rows_of(x + 3 if which == 4 else x + 1, half)
            src, dst = raw.at[rows, :], raw.at[rows, :]
        return remote(src, dst, x_send.at[which], x_land.at[which], seq=target)

    def share(which):
        if which == 6:
            return remote(patch_ref, raw.at[rows_of(x), :], d_send.at[6], d_land.at[6], seq=sibling)
        chip = x + (3, 1, 3, 1, 2, 2)[which]
        rows = rows_of(chip, (0, 1, 1, 0, 0, 1)[which])
        return remote(raw.at[rows, :], raw.at[rows, :], d_send.at[which], d_land.at[which], seq=sibling)

    def id_copy(step):
        return remote(
            id_send, id_land.at[place], i_send.at[step], i_land.at[step], seq=lax.rem(place + step, 8)
        )

    own_wrows = pl.ds(pl.multiple_of(place * 160, 32), 160)

    def wp_swap():
        columns = pl.ds(pl.multiple_of((1 - core) * 640, 128), 640)
        return remote(wproj_ref.at[:, columns], wp.at[own_wrows, :], ws_sem.at[0], ws_sem.at[1], seq=sibling)

    def wp_part(chip):
        return pl.ds(pl.multiple_of(lax.rem(chip, 4) * 320 + row_y * 80, 16), 80)

    def wp_x(dx):
        rows = wp_part(x)
        target = lax.rem(x + dx, 4) * 2 + core
        return remote(wp.at[rows, :], wp.at[rows, :], wx_sem.at[0, dx - 1], wx_sem.at[1, dx - 1], seq=target)

    def wp_y(dx, dy):
        rows = wp_part(x + 4 - dx)
        index = (dx - 1) * 3 + dy - 1
        return remote(
            wp.at[rows, :], wp.at[rows, :], wy_sem.at[0, index], wy_sem.at[1, index],
            batch=column + lax.rem(row_y + dy, 4),
        )

    id_send[...] = jnp.zeros_like(id_send)
    id_send[0:1, 0:80] = ids_ref[...]
    share(6).start()
    ring(0).start()
    ring(1).start()
    for step in range(1, 8):
        id_copy(step).start()
    wp_swap().start()
    ring(2).start()
    ring(3).start()

    wp[own_wrows, :] = wproj_ref[:, pl.ds(pl.multiple_of(core * 640, 128), 640)]
    id_land[place] = id_send[...]
    xn[0:64, :] = jnp.zeros((64, WIDTH), jnp.bfloat16)
    xn[TALL - 64 : TALL, :] = jnp.zeros((64, WIDTH), jnp.bfloat16)
    for which in range(3):
        rows = pl.ds(which * 160, 160)
        lanes = iota((160, WIDTH), 1) == iota((160, WIDTH), 0) + place * 160
        picked = jnp.sum(jnp.where(lanes, b_ref[which : which + 1, :], 0.0), axis=1, keepdims=True)
        bias[rows, :] = jnp.broadcast_to(picked, (160, 128))
    bias_col[...] = jnp.zeros_like(bias_col)
    for head in range(2):
        bias_col[head * 128 : head * 128 + 80, :] = bias[160 + head * 80 : 240 + head * 80, :]
        flipped = jnp.transpose(bias_col[head * 128 : head * 128 + 128, :])
        bias_row[:, head * 128 : head * 128 + 128] = flipped[0:8, :]
    inner = iota((512, 512), 1)
    perm[...] = onehot(iota((512, 512), 0) == (inner & 127) * 4 + (inner >> 7))

    def project(first, xrow, columns, out):
        product = dot(wt[first : first + 160, :], xn[xrow, :], ((1,), (1,)))
        out[:, columns] = (product + bias[first : first + 160, 0:1]).astype(jnp.bfloat16)

    def project_keys(rows):
        product = dot(xn[rows, :], wk[...], ((1,), (1,)))
        k[rows, :] = (product + bias_row[0:1, :]).astype(jnp.bfloat16)

    def attend(block):
        own = pl.ds(pl.multiple_of(block * 128, 128), 128)
        band = pl.ds(pl.multiple_of(block * 128, 128), 256)
        matches = id_col[band, :] == id_row[0:1, own]
        for head in range(2):
            feats = slice(head * 80, head * 80 + 80)
            scores = dot(k[band, head * 128 : head * 128 + 80], q[feats, own])
            scores = jnp.where(matches, scores, -1e30)
            peak = jnp.max(scores, axis=0, keepdims=True)
            weights = jnp.exp2((scores - peak) * SCALE)
            total = jnp.sum(weights, axis=0, keepdims=True)
            out = dot(v[feats, band], weights.astype(jnp.bfloat16))
            attn[feats, own] = (out * (1.0 / total)).astype(jnp.bfloat16)

    def normalise(chip, halves):
        gain = lanes_of(gain_ref, 0, 10)
        for at in range(2):
            for half in halves:
                first = lax.rem(chip, 4) * 640 + at * 320 + half * 160

                @pl.loop(0, 10, unroll=2)
                def _(tile):
                    start = pl.multiple_of(first + tile * 16, 16)
                    rows = raw[pl.ds(start, 16), :].astype(jnp.float32)
                    level = lax.rsqrt(jnp.mean(rows * rows, axis=1, keepdims=True) + 1e-06)
                    xn[pl.ds(pl.multiple_of(start + 64, 16), 16), :] = (rows * level * gain).astype(jnp.bfloat16)

    def take_chip(chip):
        chip = lax.rem(chip, 4)
        base = chip * 640
        project(0, pl.ds(pl.multiple_of(base + 64, 64), 640), pl.ds(pl.multiple_of(base, 128), 640), q)
        wide = pl.ds(pl.multiple_of(base + 128, 128), 512)
        project_keys(wide)
        project(320, wide, wide, v)
        for tile in range(1, 4):
            attend(chip * 5 + tile)

    def take_edge(edge):
        columns = pl.ds(pl.multiple_of(edge * 640, 128), 128)
        project_keys(columns)
        project(320, columns, columns, v)

        @pl.when(edge > 0)
        def _():
            attend(edge * 5 - 1)

        @pl.when(edge < 4)
        def _():
            attend(edge * 5)

    def chunk_of(part):
        return pl.ds(pl.multiple_of(part * 128, 128), 128)

    def feats_of(chip, at):
        return pl.ds(pl.multiple_of(lax.rem(chip, 4) * 320 + at * 160, 32), 160)

    def a_copy(dx, part):
        chip = lax.rem(x + dx, 4)
        return remote(
            pieces.at[chip, :, chunk_of(part)],
            mixed.at[feats_of(x, core), chunk_of(part)],
            a_send.at[dx - 1, part],
            a_land.at[dx - 1, part],
            seq=chip * 2 + core,
        )

    def a_share(dx, part):
        block = mixed.at[feats_of(x + 4 - dx, core), chunk_of(part)]
        return remote(block, block, f_send.at[dx, part], f_land.at[dx, part], seq=sibling)

    def late_chip(chip):
        return lax.rem(chip + 2, 4)

    def early(chip, at):
        return lax.rem(late_chip(chip) + 2 + at, 5)

    def sort_chunk(part):
        chunk = attn[:, pl.ds(pl.multiple_of(part * 512, 128), 512)]
        sorted_rows = dot(chunk, perm[...]).astype(jnp.bfloat16)
        for dest in range(4):
            pieces[dest, :, chunk_of(part)] = sorted_rows[:, dest * 128 : dest * 128 + 128]
        mixed[feats_of(x, core), chunk_of(part)] = pieces[x, :, chunk_of(part)]

    def send_chunk(part):
        for dx in (2, 1, 3):
            a_copy(dx, part).start()
        a_share(0, part).start()

    id_col[0:64, :] = jnp.full((64, 128), -1.0, jnp.float32)
    id_col[TALL - 64 : TALL, :] = jnp.full((64, 128), -1.0, jnp.float32)
    w_load.wait()
    wk[...] = jnp.zeros_like(wk)
    for head in range(2):
        wk[head * 128 : head * 128 + 80, :] = wt[160 + head * 80 : 240 + head * 80, :]
    tables(tok_ref, owner_ref, count_ref, batch, steps, jumps, owners, dests, slot, source)
    own_load.wait()
    for step in range(1, 8):
        id_copy(step).wait_recv()
    spread = iota((640, 256), 0)
    spread = onehot(jnp.where(spread < 320, spread >> 2, ((spread - 320) >> 2) + 128) == iota((640, 256), 1))
    for chip in range(4):
        units = jnp.concatenate([id_land[chip * 2, 0:1, :], id_land[chip * 2 + 1, 0:1, :]], axis=1)
        units = units.astype(jnp.float32).astype(jnp.bfloat16)
        id_row[:, chip * 640 : chip * 640 + 640] = dot(jnp.broadcast_to(units, (8, 256)), spread, ((1,), (1,)))
        id_col[chip * 640 + 64 : chip * 640 + 704, :] = dot(
            spread, jnp.broadcast_to(units, (128, 256)), ((1,), (1,))
        )
    share(6).wait_recv()
    normalise(x, (0, 1))
    take_chip(x)
    for which in (0, 1):
        ring(which).wait_recv()
        ring(which + 4).start()
        share(which).start()
    wp_swap().wait_recv()
    for dx in range(1, 4):
        wp_x(dx).start()
    share(0).wait_recv()
    share(1).wait_recv()
    normalise(x + 3, (0,))
    normalise(x + 1, (1,))
    for which in (2, 3):
        ring(which).wait_recv()
        share(which).start()
    share(2).wait_recv()
    normalise(x + 3, (1,))
    take_chip(x + 3)
    share(3).wait_recv()
    normalise(x + 1, (0,))
    take_chip(x + 1)

    @pl.loop(0, 3)
    def _(at):
        take_edge(early(x, at))

    for which in (4, 5):
        ring(which).wait_recv()
        share(which).start()

    @pl.loop(0, 3)
    def _(at):
        sort_chunk(early(x, at))

    for dx in range(1, 4):
        wp_x(dx).wait_recv()
        for dy in range(1, 4):
            wp_y(dx, dy).start()

    @pl.loop(0, 3)
    def _(at):
        send_chunk(early(x, at))

    for which in (4, 5):
        share(which).wait_recv()
    normalise(x + 2, (0, 1))
    take_chip(x + 2)

    @pl.loop(0, 2)
    def _(at):
        take_edge(late_chip(x) + at)

    @pl.loop(0, 2)
    def _(at):
        sort_chunk(late_chip(x) + at)
        send_chunk(late_chip(x) + at)

    def pass_on(dx, part):
        a_copy(dx, part).wait_recv()
        a_share(dx, part).start()

    @pl.loop(0, 3)
    def _(at):
        for dx in (1, 3, 2):
            pass_on(dx, early(x + 4 - dx, at))

    half = pl.ds(pl.multiple_of(core * 640, 128), 640)
    pick = onehot(iota((128, 512), 1) == iota((128, 512), 0) * 4 + x)

    @pl.loop(0, 5)
    def _(part):
        rows = raw[pl.ds(pl.multiple_of(part * 512, 128), 512), half]
        resid[chunk_of(part), :] = dot(pick, rows) + lanes_of(bproj_ref, core * 5, 5)

    @pl.loop(0, 2)
    def _(at):
        for dx in (1, 3, 2):
            pass_on(dx, late_chip(x + 4 - dx) + at)

    for dx in range(1, 4):
        for dy in range(1, 4):
            wp_y(dx, dy).wait_recv()

    def s_copy(part):
        return remote(
            sums_out.at[chunk_of(part), :], sums_in.at[chunk_of(part), :], s_sem.at[0, part], s_sem.at[1, part],
            seq=sibling,
        )

    @pl.loop(0, 5)
    def _(part):
        for dx in (0, 1, 3, 2):
            a_share(dx, part).wait_recv()
        rows = resid[chunk_of(part), :] + dot(mixed[:, chunk_of(part)], wp[...], ((0,), (0,)))
        resid[chunk_of(part), :] = rows
        total = jnp.sum(rows * rows, axis=1, keepdims=True)
        sums_out[chunk_of(part), :] = jnp.broadcast_to(total, (128, 128))
        s_copy(part).start()

    @pl.loop(0, 5)
    def _(part):
        s_copy(part).wait_recv()
        total = sums_out[chunk_of(part), 0:1] + sums_in[chunk_of(part), 0:1]
        level = lax.rsqrt(total * (1.0 / WIDTH) + 1e-06)
        merged_ref[chunk_of(part), :] = (resid[chunk_of(part), :] * level * lanes_of(merge_ref, core * 5, 5)).astype(jnp.bfloat16)

    def copy(step):
        return pltpu.make_async_remote_copy(
            src_ref=packed.at[step],
            dst_ref=landed.at[step],
            send_sem=send_sem.at[step],
            recv_sem=land_sem.at[step],
            device_id={"batch": lax.rem(batch + step, n_batch)},
        )

    @pl.loop(0, n_batch // PER)
    def _(part):
        wanted = iota((PER * SLOTS, GROUP), 0) + (batch + part * PER) * SLOTS
        wanted = jnp.where(wanted >= ROWS, wanted - ROWS, wanted).astype(jnp.float32)
        rows = dot(onehot(slot[0:1, :] == wanted), merged_ref[...]).astype(jnp.bfloat16)
        for inner in range(PER):
            packed[part * PER + inner] = rows[inner * SLOTS : inner * SLOTS + SLOTS]
        for inner in range(PER):
            step = part * PER + inner

            @pl.when(step > 0)
            def _():
                copy(step).start()

    landed[0] = packed[0]

    step = 0
    for count in (12, 12, 6, 2):
        marks = []
        blocks = []
        for _ in range(count):
            if step > 0:
                copy(step).wait_recv()
            blocks.append(landed[step])
            group = lax.rem(batch - step + n_batch, n_batch)
            marks.append((iota((1, SLOTS), 1) + group * SLOTS).astype(jnp.float32))
            step += 1
        marks = jnp.concatenate(marks, axis=1)
        blocks = jnp.concatenate(blocks, axis=0)
        for first in (0, GROUP):
            rows = slice(first, first + GROUP)
            placed = dot(onehot(source[rows, 0:1] == marks), blocks)
            if step > count:
                placed += total_ref[rows, :]
            if step < 32:
                total_ref[rows, :] = placed
            else:
                last = min(first + GROUP, CAP)
                cache_ref[first:last, :] = placed[: last - first].astype(jnp.bfloat16)

    @pl.loop(1, n_batch)
    def _(step):
        copy(step).wait_send()

    for which in range(6):
        ring(which).wait_send()
    for which in range(7):
        share(which).wait_send()
    for step in range(1, 8):
        id_copy(step).wait_send()
    wp_swap().wait_send()
    for dx in range(1, 4):
        wp_x(dx).wait_send()
        for dy in range(1, 4):
            wp_y(dx, dy).wait_send()

    @pl.loop(0, 5)
    def _(part):
        for dx in range(1, 4):
            a_copy(dx, part).wait_send()
        for dx in range(4):
            a_share(dx, part).wait_send()
        s_copy(part).wait_send()


def encode(*arrays):
    vmem = pl.BlockSpec(memory_space=pltpu.VMEM)
    hbm = pl.BlockSpec(memory_space=pl.ANY)
    n_batch = lax.axis_size("batch")
    dma = pltpu.SemaphoreType.DMA
    bf16, f32 = jnp.bfloat16, jnp.float32
    return pl.pallas_call(
        encode_kernel,
        out_shape=jax.ShapeDtypeStruct((CAP, GROUP), bf16),
        in_specs=[hbm, vmem, vmem, hbm] + [vmem] * (len(arrays) - 4),
        out_specs=vmem,
        scratch_shapes=[
            pltpu.VMEM((GROUP, GROUP), bf16),
            pltpu.VMEM((128, 128), f32),
            pltpu.VMEM((128, 128), f32),
            pltpu.VMEM((160, 128), f32),
            pltpu.VMEM((160, 128), jnp.int32),
            pltpu.VMEM((8, GROUP), f32),
            pltpu.VMEM((ROWS, 128), f32),
            pltpu.VMEM((n_batch, SLOTS, GROUP), bf16),
            pltpu.VMEM((n_batch, SLOTS, GROUP), bf16),
            pltpu.VMEM((ROWS, GROUP), f32),
            dma((n_batch,)), dma((n_batch,)),
            pltpu.VMEM((2560, WIDTH), bf16),
            pltpu.VMEM((TALL, WIDTH), bf16),
            pltpu.VMEM((480, WIDTH), bf16),
            pltpu.VMEM((256, WIDTH), bf16),
            pltpu.VMEM((480, 128), f32),
            pltpu.VMEM((256, 128), f32),
            pltpu.VMEM((8, 256), f32),
            pltpu.VMEM((160, 2560), bf16),
            pltpu.VMEM((TALL, 256), bf16),
            pltpu.VMEM((160, TALL), bf16),
            pltpu.VMEM((512, 512), bf16),
            pltpu.VMEM((8, 128), jnp.int32),
            pltpu.VMEM((8, 8, 128), jnp.int32),
            pltpu.VMEM((8, 2560), f32),
            pltpu.VMEM((TALL, 128), f32),
            pltpu.VMEM((160, 2560), bf16),
            pltpu.VMEM((4, 160, GROUP), bf16),
            pltpu.VMEM((WIDTH, GROUP), bf16),
            pltpu.VMEM((WIDTH, GROUP), bf16),
            pltpu.VMEM((GROUP, GROUP), f32),
            pltpu.VMEM((GROUP, 128), f32),
            pltpu.VMEM((GROUP, 128), f32),
            dma((6,)), dma((6,)), dma((7,)), dma((7,)), dma((8,)), dma((8,)),
            dma((2,)), dma((2, 3)), dma((2, 9)),
            dma((3, 5)), dma((3, 5)), dma((4, 5)), dma((4, 5)), dma((2, 5)), dma((2,)),
        ],
        compiler_params=pltpu.CompilerParams(
            collective_id=0, has_side_effects=True, vmem_limit_bytes=56 * 1024 * 1024
        ),
    )(*arrays)


def shards(
    patches, window_ids, norm_gain, w_qkv, b_qkv, w_proj, b_proj, merge_gain, token_lists, req_owner, req_counts
):
    return encode(
        patches[0],
        window_ids,
        norm_gain.reshape(10, 128),
        jnp.transpose(w_qkv, (0, 2, 1)).reshape(480, WIDTH),
        b_qkv,
        w_proj,
        b_proj.reshape(10, 128),
        merge_gain.reshape(10, 128),
        token_lists.reshape(160, 128),
        req_owner[None],
        req_counts[None],
    )[None]


def solution(mesh):
    return jax.shard_map(
        shards,
        mesh=mesh,
        in_specs=(
            P("batch", "seq", None),
            P("batch", "seq"),
            P(),
            P(None, None, "seq"),
            P(),
            P("seq", None),
            P(),
            P(),
            P(),
            P(),
            P(),
        ),
        out_specs=P("batch", None, "seq"),
        check_vma=False,
    )
```

```python
import math

import jax
import jax.numpy as jnp
from jax import lax
from jax.experimental import pallas as pl
from jax.experimental.pallas import tpu as pltpu
from jax.sharding import PartitionSpec as P

REQS = 4
WIDTH = 1280
TALL = 2688
SCALE = math.log2(math.e) / math.sqrt(80)
SLOTS = 40
GROUP = 640
MOST = 319
CAP = 1276
ROWS = 1280
PER = 8


def dot(left, right, dims=((1,), (0,))):
    return lax.dot_general(left, right, (dims, ((), ())), preferred_element_type=jnp.float32)


def iota(shape, axis):
    return lax.broadcasted_iota(jnp.int32, shape, axis)


def onehot(condition):
    return jnp.where(condition, 1.0, 0.0).astype(jnp.bfloat16)


def lanes_of(ref, first, count):
    return jnp.concatenate([ref[pl.ds(first + at, 1), :] for at in range(count)], axis=1)


def tables(tok_ref, owner_ref, count_ref, batch, steps, jumps, owners, dests, slot, source):
    f32 = jnp.float32
    me = batch.astype(f32)
    counts = count_ref[...].astype(f32)
    owner = owner_ref[...].astype(f32)

    def flip(row):
        return jnp.transpose(jnp.broadcast_to(row, (128, 128)))

    lower = iota((128, 128), 0) < iota((128, 128), 1)
    owner_down = flip(owner)
    starts = jnp.sum(jnp.where(lower, flip(counts), 0.0), axis=0, keepdims=True)
    ranks = jnp.sum(jnp.where(lower & (owner_down == owner), 1.0, 0.0), axis=0, keepdims=True)
    steps[...] = flip(starts)
    previous = jnp.where(iota((128, 128), 0) == 0, 0.0, pltpu.roll(owner_down, 1, 0))
    jumps[...] = owner_down - previous
    places = (iota((160, 128), 0) * 128 + iota((160, 128), 1)).astype(f32)

    def jump(request, held):
        return held + jnp.where(places >= steps[pl.ds(request, 1), :], jumps[pl.ds(request, 1), :], 0.0)

    owners[...] = lax.fori_loop(0, 128, jump, jnp.zeros((160, 128), f32), unroll=4)
    dest = jnp.zeros((160, 128), f32)
    for rank in range(REQS):
        chosen = (owner == me) & (ranks == rank)
        start = jnp.sum(jnp.where(chosen, starts, 0.0), axis=1, keepdims=True)
        count = jnp.sum(jnp.where(chosen, counts, 0.0), axis=1, keepdims=True)
        within = (places >= start) & (places < start + count)
        dest = dest + jnp.where(within, places - start + (MOST * rank + 1), 0.0)
    dests[...] = dest.astype(jnp.int32) - 1

    def gather(part, sums):
        rows = pl.ds(pl.multiple_of(part * 8, 8), 8)
        token = tok_ref[rows, :]
        local = token - batch * GROUP
        dest = dests[rows, :]
        owner = owners[rows, :] + 1.0
        high = (token >> 7).astype(f32) + 1.0
        low = (token & 127).astype(f32)
        down, short = iota((128, 128), 0), iota((16, 128), 0)
        group_left, group_right, own_left, own_right = [], [], [], []
        for at in range(8):
            row = slice(at, at + 1)
            group_left.append(onehot(down == (local[row] & 127)))
            group_right.append(jnp.where(short == (local[row] >> 7), owner[row], 0.0).astype(jnp.bfloat16))
            own_left.append(onehot(down == (dest[row] & 127)))
            mine = short == (dest[row] >> 7)
            own_right.append(
                jnp.concatenate([jnp.where(mine, high[row], 0.0), jnp.where(mine, low[row], 0.0)], axis=0).astype(
                    jnp.bfloat16
                )
            )
        first = dot(jnp.concatenate(group_left, axis=1), jnp.concatenate(group_right, axis=1), ((1,), (1,)))
        second = dot(jnp.concatenate(own_left, axis=1), jnp.concatenate(own_right, axis=1), ((1,), (1,)))
        return sums[0] + first, sums[1] + second

    owner_cols, token_cols = lax.fori_loop(
        0, 20, gather, (jnp.zeros((128, 16), f32), jnp.zeros((128, 32), f32))
    )
    unit = onehot(iota((128, 128), 0) == iota((128, 128), 1))
    owner_rows = dot(owner_cols.astype(jnp.bfloat16), unit, ((0,), (0,)))
    token_rows = dot(token_cols.astype(jnp.bfloat16), unit, ((0,), (0,)))

    owner_row = jnp.concatenate([owner_rows[at : at + 1] for at in range(5)], axis=1)
    before = jnp.zeros((1, GROUP), f32)
    for at in range(5):
        same = (owner_cols[:, at : at + 1] == owner_row) & (
            iota((128, GROUP), 0) + at * 128 < iota((128, GROUP), 1)
        )
        before = before + jnp.sum(jnp.where(same, 1.0, 0.0), axis=0, keepdims=True)
    slot[...] = jnp.broadcast_to((owner_row - 1.0) * SLOTS + before, (8, GROUP))

    token_row = jnp.concatenate(
        [(token_rows[at : at + 1] - 1.0) * 128 + token_rows[at + 16 : at + 17] for at in range(10)], axis=1
    )
    for at in range(10):
        high = token_cols[:, at : at + 1] - 1.0
        token = high * 128 + token_cols[:, at + 16 : at + 17]
        group = jnp.floor((high + 0.5) * 0.2)
        earlier = jnp.where((token_row < token) & (token_row >= group * GROUP), 1.0, 0.0)
        taken = jnp.sum(earlier, axis=1, keepdims=True)
        found = jnp.where(high >= 0.0, group * SLOTS + taken, -1.0)
        source[at * 128 : at * 128 + 128, :] = jnp.broadcast_to(found, (128, 128))


def encode_kernel(
    patch_ref, ids_ref, gain_ref, w_ref, b_ref, wproj_ref, bproj_ref, merge_ref, tok_ref, owner_ref, count_ref,
    cache_ref, merged_ref, steps, jumps, owners, dests, slot, source, packed, landed, total_ref, send_sem, land_sem,
    raw, xn, wt, wk, bias, bias_col, bias_row, q, k, v, perm, id_send, id_land, id_row, id_col, attn, pieces, mixed, wp, resid,
    sums_out, sums_in, x_send, x_land, d_send, d_land, i_send, i_land, ws_sem, wx_sem, wy_sem,
    a_send, a_land, f_send, f_land, s_sem, l_sem,
):
    place = lax.axis_index("seq")
    batch = lax.axis_index("batch")
    n_batch = lax.axis_size("batch")
    x, core = place // 2, place % 2
    row_y = batch % 4
    column = batch - row_y
    sibling = place + 1 - 2 * core
    right = lax.rem(x + 1, 4) * 2 + core
    left = lax.rem(x + 3, 4) * 2 + core
    own_rows = pl.ds(pl.multiple_of(place * 320, 32), 320)
    own_load = pltpu.make_async_copy(patch_ref, raw.at[own_rows, :], l_sem.at[0])
    w_load = pltpu.make_async_copy(w_ref, wt, l_sem.at[1])
    own_load.start()
    w_load.start()
    barrier = pltpu.get_barrier_semaphore()

    for step in range(1, 8):
        pl.semaphore_signal(barrier, inc=1, device_id={"seq": lax.rem(place + step, 8)})

    @pl.loop(1, n_batch)
    def _(step):
        pl.semaphore_signal(barrier, inc=1, device_id={"batch": lax.rem(batch + step, n_batch)})

    pl.semaphore_wait(barrier, 7 + n_batch - 1)

    def rows_of(chip, half=None):
        start = lax.rem(chip, 4) * 640 + core * 320
        if half is None:
            return pl.ds(pl.multiple_of(start, 32), 320)
        return pl.ds(pl.multiple_of(start + half * 160, 32), 160)

    def remote(src, dst, send, land, **device):
        return pltpu.make_async_remote_copy(
            src_ref=src, dst_ref=dst, send_sem=send, recv_sem=land, device_id=device
        )

    def ring(which):
        half = (0, 1, 1, 0, 0, 1)[which]
        target = (right, left, right, left, right, left)[which]
        if which < 4:
            src = patch_ref.at[pl.ds(half * 160, 160), :]
            dst = raw.at[rows_of(x, half), :]
        else:
            rows = rows_of(x + 3 if which == 4 else x + 1, half)
            src, dst = raw.at[rows, :], raw.at[rows, :]
        return remote(src, dst, x_send.at[which], x_land.at[which], seq=target)

    def share(which):
        if which == 6:
            return remote(patch_ref, raw.at[rows_of(x), :], d_send.at[6], d_land.at[6], seq=sibling)
        chip = x + (3, 1, 3, 1, 2, 2)[which]
        rows = rows_of(chip, (0, 1, 1, 0, 0, 1)[which])
        return remote(raw.at[rows, :], raw.at[rows, :], d_send.at[which], d_land.at[which], seq=sibling)

    def id_copy(step):
        return remote(
            id_send, id_land.at[place], i_send.at[step], i_land.at[step], seq=lax.rem(place + step, 8)
        )

    own_wrows = pl.ds(pl.multiple_of(place * 160, 32), 160)

    def wp_swap():
        columns = pl.ds(pl.multiple_of((1 - core) * 640, 128), 640)
        return remote(wproj_ref.at[:, columns], wp.at[own_wrows, :], ws_sem.at[0], ws_sem.at[1], seq=sibling)

    def wp_part(chip):
        return pl.ds(pl.multiple_of(lax.rem(chip, 4) * 320 + row_y * 80, 16), 80)

    def wp_x(dx):
        rows = wp_part(x)
        target = lax.rem(x + dx, 4) * 2 + core
        return remote(wp.at[rows, :], wp.at[rows, :], wx_sem.at[0, dx - 1], wx_sem.at[1, dx - 1], seq=target)

    def wp_y(dx, dy):
        rows = wp_part(x + 4 - dx)
        index = (dx - 1) * 3 + dy - 1
        return remote(
            wp.at[rows, :], wp.at[rows, :], wy_sem.at[0, index], wy_sem.at[1, index],
            batch=column + lax.rem(row_y + dy, 4),
        )

    id_send[...] = jnp.zeros_like(id_send)
    id_send[0:1, 0:80] = ids_ref[...]
    share(6).start()
    ring(0).start()
    ring(1).start()
    for step in range(1, 8):
        id_copy(step).start()
    wp_swap().start()
    ring(2).start()
    ring(3).start()

    wp[own_wrows, :] = wproj_ref[:, pl.ds(pl.multiple_of(core * 640, 128), 640)]
    id_land[place] = id_send[...]
    xn[0:64, :] = jnp.zeros((64, WIDTH), jnp.bfloat16)
    xn[TALL - 64 : TALL, :] = jnp.zeros((64, WIDTH), jnp.bfloat16)
    for which in range(3):
        rows = pl.ds(which * 160, 160)
        lanes = iota((160, WIDTH), 1) == iota((160, WIDTH), 0) + place * 160
        picked = jnp.sum(jnp.where(lanes, b_ref[which : which + 1, :], 0.0), axis=1, keepdims=True)
        bias[rows, :] = jnp.broadcast_to(picked, (160, 128))
    bias_col[...] = jnp.zeros_like(bias_col)
    for head in range(2):
        bias_col[head * 128 : head * 128 + 80, :] = bias[160 + head * 80 : 240 + head * 80, :]
        flipped = jnp.transpose(bias_col[head * 128 : head * 128 + 128, :])
        bias_row[:, head * 128 : head * 128 + 128] = flipped[0:8, :]
    inner = iota((512, 512), 1)
    perm[...] = onehot(iota((512, 512), 0) == (inner & 127) * 4 + (inner >> 7))

    def project(first, xrow, columns, out):
        product = dot(wt[first : first + 160, :], xn[xrow, :], ((1,), (1,)))
        out[:, columns] = (product + bias[first : first + 160, 0:1]).astype(jnp.bfloat16)

    def project_keys(rows):
        product = dot(xn[rows, :], wk[...], ((1,), (1,)))
        k[rows, :] = (product + bias_row[0:1, :]).astype(jnp.bfloat16)

    def attend(block):
        own = pl.ds(pl.multiple_of(block * 128, 128), 128)
        band = pl.ds(pl.multiple_of(block * 128, 128), 256)
        matches = id_col[band, :] == id_row[0:1, own]
        for head in range(2):
            feats = slice(head * 80, head * 80 + 80)
            scores = dot(k[band, head * 128 : head * 128 + 80], q[feats, own])
            scores = jnp.where(matches, scores, -1e30)
            peak = jnp.max(scores, axis=0, keepdims=True)
            weights = jnp.exp2((scores - peak) * SCALE)
            total = jnp.sum(weights, axis=0, keepdims=True)
            out = dot(v[feats, band], weights.astype(jnp.bfloat16))
            attn[feats, own] = (out * (1.0 / total)).astype(jnp.bfloat16)

    def normalise(chip, halves):
        gain = lanes_of(gain_ref, 0, 10)
        for at in range(2):
            for half in halves:
                first = lax.rem(chip, 4) * 640 + at * 320 + half * 160

                @pl.loop(0, 10, unroll=2)
                def _(tile):
                    start = pl.multiple_of(first + tile * 16, 16)
                    rows = raw[pl.ds(start, 16), :].astype(jnp.float32)
                    level = lax.rsqrt(jnp.mean(rows * rows, axis=1, keepdims=True) + 1e-06)
                    xn[pl.ds(pl.multiple_of(start + 64, 16), 16), :] = (rows * level * gain).astype(jnp.bfloat16)

    def take_chip(chip, edges=False):
        chip = lax.rem(chip, 4)
        base = chip * 640
        project(0, pl.ds(pl.multiple_of(base + 64, 64), 640), pl.ds(pl.multiple_of(base, 128), 640), q)
        wide = pl.ds(pl.multiple_of(base, 128), 768) if edges else pl.ds(pl.multiple_of(base + 128, 128), 512)
        project_keys(wide)
        project(320, wide, wide, v)
        for tile in range(1, 4):
            attend(chip * 5 + tile)

    def take_edge(edge, projected=False):
        if not projected:
            columns = pl.ds(pl.multiple_of(edge * 640, 128), 128)
            project_keys(columns)
            project(320, columns, columns, v)

        @pl.when(edge > 0)
        def _():
            attend(edge * 5 - 1)

        @pl.when(edge < 4)
        def _():
            attend(edge * 5)

    def chunk_of(part):
        return pl.ds(pl.multiple_of(part * 128, 128), 128)

    def feats_of(chip, at):
        return pl.ds(pl.multiple_of(lax.rem(chip, 4) * 320 + at * 160, 32), 160)

    def a_copy(dx, part):
        chip = lax.rem(x + dx, 4)
        return remote(
            pieces.at[chip, :, chunk_of(part)],
            mixed.at[feats_of(x, core), chunk_of(part)],
            a_send.at[dx - 1, part],
            a_land.at[dx - 1, part],
            seq=chip * 2 + core,
        )

    def a_share(dx, part):
        block = mixed.at[feats_of(x + 4 - dx, core), chunk_of(part)]
        return remote(block, block, f_send.at[dx, part], f_land.at[dx, part], seq=sibling)

    def late_chip(chip):
        return lax.rem(chip + 2, 4)

    def early(chip, at):
        return lax.rem(late_chip(chip) + 2 + at, 5)

    def sort_chunk(part):
        chunk = attn[:, pl.ds(pl.multiple_of(part * 512, 128), 512)]
        sorted_rows = dot(chunk, perm[...]).astype(jnp.bfloat16)
        for dest in range(4):
            pieces[dest, :, chunk_of(part)] = sorted_rows[:, dest * 128 : dest * 128 + 128]
        mixed[feats_of(x, core), chunk_of(part)] = pieces[x, :, chunk_of(part)]

    def send_chunk(part):
        for dx in (2, 1, 3):
            a_copy(dx, part).start()
        a_share(0, part).start()

    id_col[0:64, :] = jnp.full((64, 128), -1.0, jnp.float32)
    id_col[TALL - 64 : TALL, :] = jnp.full((64, 128), -1.0, jnp.float32)
    w_load.wait()
    wk[...] = jnp.zeros_like(wk)
    for head in range(2):
        wk[head * 128 : head * 128 + 80, :] = wt[160 + head * 80 : 240 + head * 80, :]
    tables(tok_ref, owner_ref, count_ref, batch, steps, jumps, owners, dests, slot, source)
    own_load.wait()
    for which in (0, 1):
        ring(which).wait_recv()
        ring(which + 4).start()
        share(which).start()
    wp_swap().wait_recv()
    for dx in range(1, 4):
        wp_x(dx).start()
    for step in range(1, 8):
        id_copy(step).wait_recv()
    spread = iota((640, 256), 0)
    spread = onehot(jnp.where(spread < 320, spread >> 2, ((spread - 320) >> 2) + 128) == iota((640, 256), 1))
    for chip in range(4):
        units = jnp.concatenate([id_land[chip * 2, 0:1, :], id_land[chip * 2 + 1, 0:1, :]], axis=1)
        units = units.astype(jnp.float32).astype(jnp.bfloat16)
        id_row[:, chip * 640 : chip * 640 + 640] = dot(jnp.broadcast_to(units, (8, 256)), spread, ((1,), (1,)))
        id_col[chip * 640 + 64 : chip * 640 + 704, :] = dot(
            spread, jnp.broadcast_to(units, (128, 256)), ((1,), (1,))
        )
    share(6).wait_recv()
    normalise(x, (0, 1))
    take_chip(x)
    share(0).wait_recv()
    share(1).wait_recv()
    normalise(x + 3, (0,))
    normalise(x + 1, (1,))
    for which in (2, 3):
        ring(which).wait_recv()
        share(which).start()
    share(2).wait_recv()
    normalise(x + 3, (1,))
    take_chip(x + 3)
    share(3).wait_recv()
    normalise(x + 1, (0,))
    take_chip(x + 1)

    @pl.loop(0, 3)
    def _(at):
        take_edge(early(x, at))

    for which in (4, 5):
        ring(which).wait_recv()
        share(which).start()

    @pl.loop(0, 3)
    def _(at):
        sort_chunk(early(x, at))

    for dx in range(1, 4):
        wp_x(dx).wait_recv()
        for dy in range(1, 4):
            wp_y(dx, dy).start()

    @pl.loop(0, 3)
    def _(at):
        send_chunk(early(x, at))

    for which in (4, 5):
        share(which).wait_recv()
    normalise(x + 2, (0, 1))
    take_chip(x + 2, True)

    @pl.loop(0, 2)
    def _(at):
        take_edge(late_chip(x) + at, True)

    @pl.loop(0, 2)
    def _(at):
        sort_chunk(late_chip(x) + at)
        send_chunk(late_chip(x) + at)

    def pass_on(dx, part):
        a_copy(dx, part).wait_recv()
        a_share(dx, part).start()

    @pl.loop(0, 3)
    def _(at):
        for dx in (1, 3, 2):
            pass_on(dx, early(x + 4 - dx, at))

    half = pl.ds(pl.multiple_of(core * 640, 128), 640)
    pick = onehot(iota((128, 512), 1) == iota((128, 512), 0) * 4 + x)

    @pl.loop(0, 5)
    def _(part):
        rows = raw[pl.ds(pl.multiple_of(part * 512, 128), 512), half]
        resid[chunk_of(part), :] = dot(pick, rows) + lanes_of(bproj_ref, core * 5, 5)

    @pl.loop(0, 2)
    def _(at):
        for dx in (1, 3, 2):
            pass_on(dx, late_chip(x + 4 - dx) + at)

    for dx in range(1, 4):
        for dy in range(1, 4):
            wp_y(dx, dy).wait_recv()

    def s_copy(part):
        return remote(
            sums_out.at[chunk_of(part), :], sums_in.at[chunk_of(part), :], s_sem.at[0, part], s_sem.at[1, part],
            seq=sibling,
        )

    @pl.loop(0, 5)
    def _(part):
        for dx in (0, 1, 3, 2):
            a_share(dx, part).wait_recv()
        rows = resid[chunk_of(part), :] + dot(mixed[:, chunk_of(part)], wp[...], ((0,), (0,)))
        resid[chunk_of(part), :] = rows
        total = jnp.sum(rows * rows, axis=1, keepdims=True)
        sums_out[chunk_of(part), :] = jnp.broadcast_to(total, (128, 128))
        s_copy(part).start()

    @pl.loop(0, 5)
    def _(part):
        s_copy(part).wait_recv()
        total = sums_out[chunk_of(part), 0:1] + sums_in[chunk_of(part), 0:1]
        level = lax.rsqrt(total * (1.0 / WIDTH) + 1e-06)
        merged_ref[chunk_of(part), :] = (resid[chunk_of(part), :] * level * lanes_of(merge_ref, core * 5, 5)).astype(jnp.bfloat16)

    def copy(step):
        return pltpu.make_async_remote_copy(
            src_ref=packed.at[step],
            dst_ref=landed.at[step],
            send_sem=send_sem.at[step],
            recv_sem=land_sem.at[step],
            device_id={"batch": lax.rem(batch + step, n_batch)},
        )

    @pl.loop(0, n_batch // PER)
    def _(part):
        wanted = iota((PER * SLOTS, GROUP), 0) + (batch + part * PER) * SLOTS
        wanted = jnp.where(wanted >= ROWS, wanted - ROWS, wanted).astype(jnp.float32)
        rows = dot(onehot(slot[0:1, :] == wanted), merged_ref[...]).astype(jnp.bfloat16)
        for inner in range(PER):
            packed[part * PER + inner] = rows[inner * SLOTS : inner * SLOTS + SLOTS]
        for inner in range(PER):
            step = part * PER + inner

            @pl.when(step > 0)
            def _():
                copy(step).start()

    landed[0] = packed[0]

    step = 0
    for count in (12, 12, 6, 2):
        marks = []
        blocks = []
        for _ in range(count):
            if step > 0:
                copy(step).wait_recv()
            blocks.append(landed[step])
            group = lax.rem(batch - step + n_batch, n_batch)
            marks.append((iota((1, SLOTS), 1) + group * SLOTS).astype(jnp.float32))
            step += 1
        marks = jnp.concatenate(marks, axis=1)
        blocks = jnp.concatenate(blocks, axis=0)
        for first in (0, GROUP):
            rows = slice(first, first + GROUP)
            placed = dot(onehot(source[rows, 0:1] == marks), blocks)
            if step > count:
                placed += total_ref[rows, :]
            if step < 32:
                total_ref[rows, :] = placed
            else:
                last = min(first + GROUP, CAP)
                cache_ref[first:last, :] = placed[: last - first].astype(jnp.bfloat16)

    @pl.loop(1, n_batch)
    def _(step):
        copy(step).wait_send()

    for which in range(6):
        ring(which).wait_send()
    for which in range(7):
        share(which).wait_send()
    for step in range(1, 8):
        id_copy(step).wait_send()
    wp_swap().wait_send()
    for dx in range(1, 4):
        wp_x(dx).wait_send()
        for dy in range(1, 4):
            wp_y(dx, dy).wait_send()

    @pl.loop(0, 5)
    def _(part):
        for dx in range(1, 4):
            a_copy(dx, part).wait_send()
        for dx in range(4):
            a_share(dx, part).wait_send()
        s_copy(part).wait_send()


def encode(*arrays):
    vmem = pl.BlockSpec(memory_space=pltpu.VMEM)
    hbm = pl.BlockSpec(memory_space=pl.ANY)
    n_batch = lax.axis_size("batch")
    dma = pltpu.SemaphoreType.DMA
    bf16, f32 = jnp.bfloat16, jnp.float32
    return pl.pallas_call(
        encode_kernel,
        out_shape=jax.ShapeDtypeStruct((CAP, GROUP), bf16),
        in_specs=[hbm, vmem, vmem, hbm] + [vmem] * (len(arrays) - 4),
        out_specs=vmem,
        scratch_shapes=[
            pltpu.VMEM((GROUP, GROUP), bf16),
            pltpu.VMEM((128, 128), f32),
            pltpu.VMEM((128, 128), f32),
            pltpu.VMEM((160, 128), f32),
            pltpu.VMEM((160, 128), jnp.int32),
            pltpu.VMEM((8, GROUP), f32),
            pltpu.VMEM((ROWS, 128), f32),
            pltpu.VMEM((n_batch, SLOTS, GROUP), bf16),
            pltpu.VMEM((n_batch, SLOTS, GROUP), bf16),
            pltpu.VMEM((ROWS, GROUP), f32),
            dma((n_batch,)), dma((n_batch,)),
            pltpu.VMEM((2560, WIDTH), bf16),
            pltpu.VMEM((TALL, WIDTH), bf16),
            pltpu.VMEM((480, WIDTH), bf16),
            pltpu.VMEM((256, WIDTH), bf16),
            pltpu.VMEM((480, 128), f32),
            pltpu.VMEM((256, 128), f32),
            pltpu.VMEM((8, 256), f32),
            pltpu.VMEM((160, 2560), bf16),
            pltpu.VMEM((TALL, 256), bf16),
            pltpu.VMEM((160, TALL), bf16),
            pltpu.VMEM((512, 512), bf16),
            pltpu.VMEM((8, 128), jnp.int32),
            pltpu.VMEM((8, 8, 128), jnp.int32),
            pltpu.VMEM((8, 2560), f32),
            pltpu.VMEM((TALL, 128), f32),
            pltpu.VMEM((160, 2560), bf16),
            pltpu.VMEM((4, 160, GROUP), bf16),
            pltpu.VMEM((WIDTH, GROUP), bf16),
            pltpu.VMEM((WIDTH, GROUP), bf16),
            pltpu.VMEM((GROUP, GROUP), f32),
            pltpu.VMEM((GROUP, 128), f32),
            pltpu.VMEM((GROUP, 128), f32),
            dma((6,)), dma((6,)), dma((7,)), dma((7,)), dma((8,)), dma((8,)),
            dma((2,)), dma((2, 3)), dma((2, 9)),
            dma((3, 5)), dma((3, 5)), dma((4, 5)), dma((4, 5)), dma((2, 5)), dma((2,)),
        ],
        compiler_params=pltpu.CompilerParams(
            collective_id=0, has_side_effects=True, vmem_limit_bytes=56 * 1024 * 1024
        ),
    )(*arrays)


def shards(
    patches, window_ids, norm_gain, w_qkv, b_qkv, w_proj, b_proj, merge_gain, token_lists, req_owner, req_counts
):
    return encode(
        patches[0],
        window_ids,
        norm_gain.reshape(10, 128),
        jnp.transpose(w_qkv, (0, 2, 1)).reshape(480, WIDTH),
        b_qkv,
        w_proj,
        b_proj.reshape(10, 128),
        merge_gain.reshape(10, 128),
        token_lists.reshape(160, 128),
        req_owner[None],
        req_counts[None],
    )[None]


def solution(mesh):
    return jax.shard_map(
        shards,
        mesh=mesh,
        in_specs=(
            P("batch", "seq", None),
            P("batch", "seq"),
            P(),
            P(None, None, "seq"),
            P(),
            P("seq", None),
            P(),
            P(),
            P(),
            P(),
            P(),
        ),
        out_specs=P("batch", None, "seq"),
        check_vma=False,
    )
```

```python
import math

import jax
import jax.numpy as jnp
from jax import lax
from jax.experimental import pallas as pl
from jax.experimental.pallas import tpu as pltpu
from jax.sharding import PartitionSpec as P

REQS = 4
WIDTH = 1280
TALL = 2688
SCALE = math.log2(math.e) / math.sqrt(80)
SLOTS = 40
GROUP = 640
MOST = 319
CAP = 1276
ROWS = 1280
PER = 8


def dot(left, right, dims=((1,), (0,))):
    return lax.dot_general(left, right, (dims, ((), ())), preferred_element_type=jnp.float32)


def iota(shape, axis):
    return lax.broadcasted_iota(jnp.int32, shape, axis)


def onehot(condition):
    return jnp.where(condition, 1.0, 0.0).astype(jnp.bfloat16)


def lanes_of(ref, first, count):
    return jnp.concatenate([ref[pl.ds(first + at, 1), :] for at in range(count)], axis=1)


def tables(tok_ref, owner_ref, count_ref, batch, steps, jumps, owners, dests, slot, source):
    f32 = jnp.float32
    me = batch.astype(f32)
    counts = count_ref[...].astype(f32)
    owner = owner_ref[...].astype(f32)

    def flip(row):
        return jnp.transpose(jnp.broadcast_to(row, (128, 128)))

    lower = iota((128, 128), 0) < iota((128, 128), 1)
    owner_down = flip(owner)
    starts = jnp.sum(jnp.where(lower, flip(counts), 0.0), axis=0, keepdims=True)
    ranks = jnp.sum(jnp.where(lower & (owner_down == owner), 1.0, 0.0), axis=0, keepdims=True)
    steps[...] = flip(starts)
    previous = jnp.where(iota((128, 128), 0) == 0, 0.0, pltpu.roll(owner_down, 1, 0))
    jumps[...] = owner_down - previous
    places = (iota((160, 128), 0) * 128 + iota((160, 128), 1)).astype(f32)

    def jump(request, held):
        return held + jnp.where(places >= steps[pl.ds(request, 1), :], jumps[pl.ds(request, 1), :], 0.0)

    owners[...] = lax.fori_loop(0, 128, jump, jnp.zeros((160, 128), f32), unroll=4)
    dest = jnp.zeros((160, 128), f32)
    for rank in range(REQS):
        chosen = (owner == me) & (ranks == rank)
        start = jnp.sum(jnp.where(chosen, starts, 0.0), axis=1, keepdims=True)
        count = jnp.sum(jnp.where(chosen, counts, 0.0), axis=1, keepdims=True)
        within = (places >= start) & (places < start + count)
        dest = dest + jnp.where(within, places - start + (MOST * rank + 1), 0.0)
    dests[...] = dest.astype(jnp.int32) - 1

    def gather(part, sums):
        rows = pl.ds(pl.multiple_of(part * 8, 8), 8)
        token = tok_ref[rows, :]
        local = token - batch * GROUP
        dest = dests[rows, :]
        owner = owners[rows, :] + 1.0
        high = (token >> 7).astype(f32) + 1.0
        low = (token & 127).astype(f32)
        down, short = iota((128, 128), 0), iota((16, 128), 0)
        group_left, group_right, own_left, own_right = [], [], [], []
        for at in range(8):
            row = slice(at, at + 1)
            group_left.append(onehot(down == (local[row] & 127)))
            group_right.append(jnp.where(short == (local[row] >> 7), owner[row], 0.0).astype(jnp.bfloat16))
            own_left.append(onehot(down == (dest[row] & 127)))
            mine = short == (dest[row] >> 7)
            own_right.append(
                jnp.concatenate([jnp.where(mine, high[row], 0.0), jnp.where(mine, low[row], 0.0)], axis=0).astype(
                    jnp.bfloat16
                )
            )
        first = dot(jnp.concatenate(group_left, axis=1), jnp.concatenate(group_right, axis=1), ((1,), (1,)))
        second = dot(jnp.concatenate(own_left, axis=1), jnp.concatenate(own_right, axis=1), ((1,), (1,)))
        return sums[0] + first, sums[1] + second

    owner_cols, token_cols = lax.fori_loop(
        0, 20, gather, (jnp.zeros((128, 16), f32), jnp.zeros((128, 32), f32))
    )
    unit = onehot(iota((128, 128), 0) == iota((128, 128), 1))
    owner_rows = dot(owner_cols.astype(jnp.bfloat16), unit, ((0,), (0,)))
    token_rows = dot(token_cols.astype(jnp.bfloat16), unit, ((0,), (0,)))

    owner_row = jnp.concatenate([owner_rows[at : at + 1] for at in range(5)], axis=1)
    before = jnp.zeros((1, GROUP), f32)
    for at in range(5):
        same = (owner_cols[:, at : at + 1] == owner_row) & (
            iota((128, GROUP), 0) + at * 128 < iota((128, GROUP), 1)
        )
        before = before + jnp.sum(jnp.where(same, 1.0, 0.0), axis=0, keepdims=True)
    slot[...] = jnp.broadcast_to((owner_row - 1.0) * SLOTS + before, (8, GROUP))

    token_row = jnp.concatenate(
        [(token_rows[at : at + 1] - 1.0) * 128 + token_rows[at + 16 : at + 17] for at in range(10)], axis=1
    )
    for at in range(10):
        high = token_cols[:, at : at + 1] - 1.0
        token = high * 128 + token_cols[:, at + 16 : at + 17]
        group = jnp.floor((high + 0.5) * 0.2)
        earlier = jnp.where((token_row < token) & (token_row >= group * GROUP), 1.0, 0.0)
        taken = jnp.sum(earlier, axis=1, keepdims=True)
        found = jnp.where(high >= 0.0, group * SLOTS + taken, -1.0)
        source[at * 128 : at * 128 + 128, :] = jnp.broadcast_to(found, (128, 128))


def encode_kernel(
    patch_ref, ids_ref, gain_ref, w_ref, b_ref, wproj_ref, bproj_ref, merge_ref, tok_ref, owner_ref, count_ref,
    cache_ref, merged_ref, steps, jumps, owners, dests, slot, source, packed, landed, total_ref, send_sem, land_sem,
    raw, xn, wt, wk, bias, bias_col, bias_row, q, k, v, perm, id_send, id_land, id_row, id_col, attn, pieces, mixed, wp, resid,
    sums_out, sums_in, x_send, x_land, d_send, d_land, i_send, i_land, ws_sem, wx_sem, wy_sem,
    a_send, a_land, f_send, f_land, s_sem, l_sem,
):
    place = lax.axis_index("seq")
    batch = lax.axis_index("batch")
    n_batch = lax.axis_size("batch")
    x, core = place // 2, place % 2
    row_y = batch % 4
    column = batch - row_y
    sibling = place + 1 - 2 * core
    right = lax.rem(x + 1, 4) * 2 + core
    left = lax.rem(x + 3, 4) * 2 + core
    own_rows = pl.ds(pl.multiple_of(place * 320, 32), 320)
    own_load = pltpu.make_async_copy(patch_ref, raw.at[own_rows, :], l_sem.at[0])
    w_load = pltpu.make_async_copy(w_ref, wt, l_sem.at[1])
    own_load.start()
    w_load.start()
    barrier = pltpu.get_barrier_semaphore()

    for step in range(1, 8):
        pl.semaphore_signal(barrier, inc=1, device_id={"seq": lax.rem(place + step, 8)})

    @pl.loop(1, n_batch)
    def _(step):
        pl.semaphore_signal(barrier, inc=1, device_id={"batch": lax.rem(batch + step, n_batch)})

    pl.semaphore_wait(barrier, 7 + n_batch - 1)

    def rows_of(chip, half=None):
        start = lax.rem(chip, 4) * 640 + core * 320
        if half is None:
            return pl.ds(pl.multiple_of(start, 32), 320)
        return pl.ds(pl.multiple_of(start + half * 160, 32), 160)

    def remote(src, dst, send, land, **device):
        return pltpu.make_async_remote_copy(
            src_ref=src, dst_ref=dst, send_sem=send, recv_sem=land, device_id=device
        )

    def ring(which):
        half = (0, 1, 1, 0, 0, 1)[which]
        target = (right, left, right, left, right, left)[which]
        if which < 4:
            src = patch_ref.at[pl.ds(half * 160, 160), :]
            dst = raw.at[rows_of(x, half), :]
        else:
            rows = rows_of(x + 3 if which == 4 else x + 1, half)
            src, dst = raw.at[rows, :], raw.at[rows, :]
        return remote(src, dst, x_send.at[which], x_land.at[which], seq=target)

    def share(which):
        if which == 6:
            return remote(patch_ref, raw.at[rows_of(x), :], d_send.at[6], d_land.at[6], seq=sibling)
        chip = x + (3, 1, 3, 1, 2, 2)[which]
        rows = rows_of(chip, (0, 1, 1, 0, 0, 1)[which])
        return remote(raw.at[rows, :], raw.at[rows, :], d_send.at[which], d_land.at[which], seq=sibling)

    def id_copy(step):
        return remote(
            id_send, id_land.at[place], i_send.at[step], i_land.at[step], seq=lax.rem(place + step, 8)
        )

    own_wrows = pl.ds(pl.multiple_of(place * 160, 32), 160)

    def wp_swap():
        columns = pl.ds(pl.multiple_of((1 - core) * 640, 128), 640)
        return remote(wproj_ref.at[:, columns], wp.at[own_wrows, :], ws_sem.at[0], ws_sem.at[1], seq=sibling)

    def wp_part(chip):
        return pl.ds(pl.multiple_of(lax.rem(chip, 4) * 320 + row_y * 80, 16), 80)

    def wp_x(dx):
        rows = wp_part(x)
        target = lax.rem(x + dx, 4) * 2 + core
        return remote(wp.at[rows, :], wp.at[rows, :], wx_sem.at[0, dx - 1], wx_sem.at[1, dx - 1], seq=target)

    def wp_y(dx, dy):
        rows = wp_part(x + 4 - dx)
        index = (dx - 1) * 3 + dy - 1
        return remote(
            wp.at[rows, :], wp.at[rows, :], wy_sem.at[0, index], wy_sem.at[1, index],
            batch=column + lax.rem(row_y + dy, 4),
        )

    id_send[...] = jnp.zeros_like(id_send)
    id_send[0:1, 0:80] = ids_ref[...]
    share(6).start()
    ring(0).start()
    ring(1).start()
    for step in range(1, 8):
        id_copy(step).start()
    wp_swap().start()
    ring(2).start()
    ring(3).start()

    wp[own_wrows, :] = wproj_ref[:, pl.ds(pl.multiple_of(core * 640, 128), 640)]
    id_land[place] = id_send[...]
    xn[0:64, :] = jnp.zeros((64, WIDTH), jnp.bfloat16)
    xn[TALL - 64 : TALL, :] = jnp.zeros((64, WIDTH), jnp.bfloat16)
    for which in range(3):
        rows = pl.ds(which * 160, 160)
        lanes = iota((160, WIDTH), 1) == iota((160, WIDTH), 0) + place * 160
        picked = jnp.sum(jnp.where(lanes, b_ref[which : which + 1, :], 0.0), axis=1, keepdims=True)
        bias[rows, :] = jnp.broadcast_to(picked, (160, 128))
    bias_col[...] = jnp.zeros_like(bias_col)
    for head in range(2):
        bias_col[head * 128 : head * 128 + 80, :] = bias[160 + head * 80 : 240 + head * 80, :]
        flipped = jnp.transpose(bias_col[head * 128 : head * 128 + 128, :])
        bias_row[:, head * 128 : head * 128 + 128] = flipped[0:8, :]
    inner = iota((512, 512), 1)
    perm[...] = onehot(iota((512, 512), 0) == (inner & 127) * 4 + (inner >> 7))

    def project(first, xrow, columns, out):
        product = dot(wt[first : first + 160, :], xn[xrow, :], ((1,), (1,)))
        out[:, columns] = (product + bias[first : first + 160, 0:1]).astype(jnp.bfloat16)

    def project_keys(rows):
        product = dot(xn[rows, :], wk[...], ((1,), (1,)))
        k[rows, :] = (product + bias_row[0:1, :]).astype(jnp.bfloat16)

    def attend(block):
        own = pl.ds(pl.multiple_of(block * 128, 128), 128)
        band = pl.ds(pl.multiple_of(block * 128, 128), 256)
        matches = id_col[band, :] == id_row[0:1, own]
        for head in range(2):
            feats = slice(head * 80, head * 80 + 80)
            scores = dot(k[band, head * 128 : head * 128 + 80], q[feats, own])
            scores = jnp.where(matches, scores, -1e30)
            peak = jnp.max(scores, axis=0, keepdims=True)
            weights = jnp.exp2((scores - peak) * SCALE)
            total = jnp.sum(weights, axis=0, keepdims=True)
            out = dot(v[feats, band], weights.astype(jnp.bfloat16))
            attn[feats, own] = (out * (1.0 / total)).astype(jnp.bfloat16)

    def normalise(chip, halves):
        gain = lanes_of(gain_ref, 0, 10)
        for at in range(2):
            for half in halves:
                first = lax.rem(chip, 4) * 640 + at * 320 + half * 160

                @pl.loop(0, 10, unroll=2)
                def _(tile):
                    start = pl.multiple_of(first + tile * 16, 16)
                    rows = raw[pl.ds(start, 16), :].astype(jnp.float32)
                    level = lax.rsqrt(jnp.mean(rows * rows, axis=1, keepdims=True) + 1e-06)
                    xn[pl.ds(pl.multiple_of(start + 64, 16), 16), :] = (rows * level * gain).astype(jnp.bfloat16)

    def take_chip(chip, edges=False):
        chip = lax.rem(chip, 4)
        base = chip * 640
        project(0, pl.ds(pl.multiple_of(base + 64, 64), 640), pl.ds(pl.multiple_of(base, 128), 640), q)
        wide = pl.ds(pl.multiple_of(base, 128), 768) if edges else pl.ds(pl.multiple_of(base + 128, 128), 512)
        project_keys(wide)
        project(320, wide, wide, v)
        for tile in range(1, 4):
            attend(chip * 5 + tile)

    def take_edge(edge, projected=False):
        if not projected:
            columns = pl.ds(pl.multiple_of(edge * 640, 128), 128)
            project_keys(columns)
            project(320, columns, columns, v)

        @pl.when(edge > 0)
        def _():
            attend(edge * 5 - 1)

        @pl.when(edge < 4)
        def _():
            attend(edge * 5)

    def chunk_of(part):
        return pl.ds(pl.multiple_of(part * 128, 128), 128)

    def feats_of(chip, at):
        return pl.ds(pl.multiple_of(lax.rem(chip, 4) * 320 + at * 160, 32), 160)

    def a_copy(dx, part):
        chip = lax.rem(x + dx, 4)
        return remote(
            pieces.at[chip, :, chunk_of(part)],
            mixed.at[feats_of(x, core), chunk_of(part)],
            a_send.at[dx - 1, part],
            a_land.at[dx - 1, part],
            seq=chip * 2 + core,
        )

    def a_share(dx, part):
        block = mixed.at[feats_of(x + 4 - dx, core), chunk_of(part)]
        return remote(block, block, f_send.at[dx, part], f_land.at[dx, part], seq=sibling)

    def late_chip(chip):
        return lax.rem(chip + 2, 4)

    def early(chip, at):
        return lax.rem(late_chip(chip) + 2 + at, 5)

    def sort_chunk(part):
        chunk = attn[:, pl.ds(pl.multiple_of(part * 512, 128), 512)]
        sorted_rows = dot(chunk, perm[...]).astype(jnp.bfloat16)
        for dest in range(4):
            pieces[dest, :, chunk_of(part)] = sorted_rows[:, dest * 128 : dest * 128 + 128]
        mixed[feats_of(x, core), chunk_of(part)] = pieces[x, :, chunk_of(part)]

    def send_chunk(part):
        for dx in (2, 1, 3):
            a_copy(dx, part).start()
        a_share(0, part).start()

    id_col[0:64, :] = jnp.full((64, 128), -1.0, jnp.float32)
    id_col[TALL - 64 : TALL, :] = jnp.full((64, 128), -1.0, jnp.float32)
    w_load.wait()
    wk[...] = jnp.zeros_like(wk)
    for head in range(2):
        wk[head * 128 : head * 128 + 80, :] = wt[160 + head * 80 : 240 + head * 80, :]
    tables(tok_ref, owner_ref, count_ref, batch, steps, jumps, owners, dests, slot, source)
    own_load.wait()
    for which in (0, 1):
        ring(which).wait_recv()
        ring(which + 4).start()
        share(which).start()
    wp_swap().wait_recv()
    for dx in range(1, 4):
        wp_x(dx).start()
    for step in range(1, 8):
        id_copy(step).wait_recv()
    spread = iota((640, 256), 0)
    spread = onehot(jnp.where(spread < 320, spread >> 2, ((spread - 320) >> 2) + 128) == iota((640, 256), 1))
    for chip in range(4):
        units = jnp.concatenate([id_land[chip * 2, 0:1, :], id_land[chip * 2 + 1, 0:1, :]], axis=1)
        units = units.astype(jnp.float32).astype(jnp.bfloat16)
        id_row[:, chip * 640 : chip * 640 + 640] = dot(jnp.broadcast_to(units, (8, 256)), spread, ((1,), (1,)))
        id_col[chip * 640 + 64 : chip * 640 + 704, :] = dot(
            spread, jnp.broadcast_to(units, (128, 256)), ((1,), (1,))
        )
    share(6).wait_recv()
    normalise(x, (0, 1))
    take_chip(x)
    share(0).wait_recv()
    share(1).wait_recv()
    normalise(x + 3, (0,))
    normalise(x + 1, (1,))
    for which in (2, 3):
        ring(which).wait_recv()
        share(which).start()
    share(2).wait_recv()
    normalise(x + 3, (1,))
    take_chip(x + 3)
    share(3).wait_recv()
    normalise(x + 1, (0,))
    take_chip(x + 1)

    @pl.loop(0, 3)
    def _(at):
        take_edge(early(x, at))

    for which in (4, 5):
        ring(which).wait_recv()
        share(which).start()

    @pl.loop(0, 3)
    def _(at):
        sort_chunk(early(x, at))

    for dx in range(1, 4):
        wp_x(dx).wait_recv()
        for dy in range(1, 4):
            wp_y(dx, dy).start()

    @pl.loop(0, 3)
    def _(at):
        send_chunk(early(x, at))

    for which in (4, 5):
        share(which).wait_recv()
    normalise(x + 2, (0, 1))
    take_chip(x + 2, True)

    @pl.loop(0, 2)
    def _(at):
        take_edge(late_chip(x) + at, True)

    def pass_on(dx, part):
        a_copy(dx, part).wait_recv()
        a_share(dx, part).start()

    @pl.loop(0, 3)
    def _(at):
        for dx in (1, 3, 2):
            pass_on(dx, early(x + 4 - dx, at))

    @pl.loop(0, 2)
    def _(at):
        sort_chunk(late_chip(x) + at)
        send_chunk(late_chip(x) + at)

    half = pl.ds(pl.multiple_of(core * 640, 128), 640)
    pick = onehot(iota((128, 512), 1) == iota((128, 512), 0) * 4 + x)

    @pl.loop(0, 5)
    def _(part):
        rows = raw[pl.ds(pl.multiple_of(part * 512, 128), 512), half]
        resid[chunk_of(part), :] = dot(pick, rows) + lanes_of(bproj_ref, core * 5, 5)

    @pl.loop(0, 2)
    def _(at):
        for dx in (1, 3, 2):
            pass_on(dx, late_chip(x + 4 - dx) + at)

    for dx in range(1, 4):
        for dy in range(1, 4):
            wp_y(dx, dy).wait_recv()

    def s_copy(part):
        return remote(
            sums_out.at[chunk_of(part), :], sums_in.at[chunk_of(part), :], s_sem.at[0, part], s_sem.at[1, part],
            seq=sibling,
        )

    @pl.loop(0, 5)
    def _(part):
        for dx in (0, 1, 3, 2):
            a_share(dx, part).wait_recv()
        rows = resid[chunk_of(part), :] + dot(mixed[:, chunk_of(part)], wp[...], ((0,), (0,)))
        resid[chunk_of(part), :] = rows
        total = jnp.sum(rows * rows, axis=1, keepdims=True)
        sums_out[chunk_of(part), :] = jnp.broadcast_to(total, (128, 128))
        s_copy(part).start()

    @pl.loop(0, 5)
    def _(part):
        s_copy(part).wait_recv()
        total = sums_out[chunk_of(part), 0:1] + sums_in[chunk_of(part), 0:1]
        level = lax.rsqrt(total * (1.0 / WIDTH) + 1e-06)
        merged_ref[chunk_of(part), :] = (resid[chunk_of(part), :] * level * lanes_of(merge_ref, core * 5, 5)).astype(jnp.bfloat16)

    def copy(step):
        return pltpu.make_async_remote_copy(
            src_ref=packed.at[step],
            dst_ref=landed.at[step],
            send_sem=send_sem.at[step],
            recv_sem=land_sem.at[step],
            device_id={"batch": lax.rem(batch + step, n_batch)},
        )

    @pl.loop(0, n_batch // PER)
    def _(part):
        wanted = iota((PER * SLOTS, GROUP), 0) + (batch + part * PER) * SLOTS
        wanted = jnp.where(wanted >= ROWS, wanted - ROWS, wanted).astype(jnp.float32)
        rows = dot(onehot(slot[0:1, :] == wanted), merged_ref[...]).astype(jnp.bfloat16)
        for inner in range(PER):
            packed[part * PER + inner] = rows[inner * SLOTS : inner * SLOTS + SLOTS]
        for inner in range(PER):
            step = part * PER + inner

            @pl.when(step > 0)
            def _():
                copy(step).start()

    landed[0] = packed[0]

    step = 0
    for count in (12, 12, 6, 2):
        marks = []
        blocks = []
        for _ in range(count):
            if step > 0:
                copy(step).wait_recv()
            blocks.append(landed[step])
            group = lax.rem(batch - step + n_batch, n_batch)
            marks.append((iota((1, SLOTS), 1) + group * SLOTS).astype(jnp.float32))
            step += 1
        marks = jnp.concatenate(marks, axis=1)
        blocks = jnp.concatenate(blocks, axis=0)
        for first in (0, GROUP):
            rows = slice(first, first + GROUP)
            placed = dot(onehot(source[rows, 0:1] == marks), blocks)
            if step > count:
                placed += total_ref[rows, :]
            if step < 32:
                total_ref[rows, :] = placed
            else:
                last = min(first + GROUP, CAP)
                cache_ref[first:last, :] = placed[: last - first].astype(jnp.bfloat16)

    @pl.loop(1, n_batch)
    def _(step):
        copy(step).wait_send()

    for which in range(6):
        ring(which).wait_send()
    for which in range(7):
        share(which).wait_send()
    for step in range(1, 8):
        id_copy(step).wait_send()
    wp_swap().wait_send()
    for dx in range(1, 4):
        wp_x(dx).wait_send()
        for dy in range(1, 4):
            wp_y(dx, dy).wait_send()

    @pl.loop(0, 5)
    def _(part):
        for dx in range(1, 4):
            a_copy(dx, part).wait_send()
        for dx in range(4):
            a_share(dx, part).wait_send()
        s_copy(part).wait_send()


def encode(*arrays):
    vmem = pl.BlockSpec(memory_space=pltpu.VMEM)
    hbm = pl.BlockSpec(memory_space=pl.ANY)
    n_batch = lax.axis_size("batch")
    dma = pltpu.SemaphoreType.DMA
    bf16, f32 = jnp.bfloat16, jnp.float32
    return pl.pallas_call(
        encode_kernel,
        out_shape=jax.ShapeDtypeStruct((CAP, GROUP), bf16),
        in_specs=[hbm, vmem, vmem, hbm] + [vmem] * (len(arrays) - 4),
        out_specs=vmem,
        scratch_shapes=[
            pltpu.VMEM((GROUP, GROUP), bf16),
            pltpu.VMEM((128, 128), f32),
            pltpu.VMEM((128, 128), f32),
            pltpu.VMEM((160, 128), f32),
            pltpu.VMEM((160, 128), jnp.int32),
            pltpu.VMEM((8, GROUP), f32),
            pltpu.VMEM((ROWS, 128), f32),
            pltpu.VMEM((n_batch, SLOTS, GROUP), bf16),
            pltpu.VMEM((n_batch, SLOTS, GROUP), bf16),
            pltpu.VMEM((ROWS, GROUP), f32),
            dma((n_batch,)), dma((n_batch,)),
            pltpu.VMEM((2560, WIDTH), bf16),
            pltpu.VMEM((TALL, WIDTH), bf16),
            pltpu.VMEM((480, WIDTH), bf16),
            pltpu.VMEM((256, WIDTH), bf16),
            pltpu.VMEM((480, 128), f32),
            pltpu.VMEM((256, 128), f32),
            pltpu.VMEM((8, 256), f32),
            pltpu.VMEM((160, 2560), bf16),
            pltpu.VMEM((TALL, 256), bf16),
            pltpu.VMEM((160, TALL), bf16),
            pltpu.VMEM((512, 512), bf16),
            pltpu.VMEM((8, 128), jnp.int32),
            pltpu.VMEM((8, 8, 128), jnp.int32),
            pltpu.VMEM((8, 2560), f32),
            pltpu.VMEM((TALL, 128), f32),
            pltpu.VMEM((160, 2560), bf16),
            pltpu.VMEM((4, 160, GROUP), bf16),
            pltpu.VMEM((WIDTH, GROUP), bf16),
            pltpu.VMEM((WIDTH, GROUP), bf16),
            pltpu.VMEM((GROUP, GROUP), f32),
            pltpu.VMEM((GROUP, 128), f32),
            pltpu.VMEM((GROUP, 128), f32),
            dma((6,)), dma((6,)), dma((7,)), dma((7,)), dma((8,)), dma((8,)),
            dma((2,)), dma((2, 3)), dma((2, 9)),
            dma((3, 5)), dma((3, 5)), dma((4, 5)), dma((4, 5)), dma((2, 5)), dma((2,)),
        ],
        compiler_params=pltpu.CompilerParams(
            collective_id=0, has_side_effects=True, vmem_limit_bytes=56 * 1024 * 1024
        ),
    )(*arrays)


def shards(
    patches, window_ids, norm_gain, w_qkv, b_qkv, w_proj, b_proj, merge_gain, token_lists, req_owner, req_counts
):
    return encode(
        patches[0],
        window_ids,
        norm_gain.reshape(10, 128),
        jnp.transpose(w_qkv, (0, 2, 1)).reshape(480, WIDTH),
        b_qkv,
        w_proj,
        b_proj.reshape(10, 128),
        merge_gain.reshape(10, 128),
        token_lists.reshape(160, 128),
        req_owner[None],
        req_counts[None],
    )[None]


def solution(mesh):
    return jax.shard_map(
        shards,
        mesh=mesh,
        in_specs=(
            P("batch", "seq", None),
            P("batch", "seq"),
            P(),
            P(None, None, "seq"),
            P(),
            P("seq", None),
            P(),
            P(),
            P(),
            P(),
            P(),
        ),
        out_specs=P("batch", None, "seq"),
        check_vma=False,
    )
```
